32 devices in a mesh: groups: 2 (over y), ka: 4 (over x, core), pw: 4 (over z).
Axes of the slice: x: 2, y: 2, z: 4, core: 2. Of those that a mesh axis runs over, the one named last changes fastest.
Arguments:
- coefficients: bfloat16 [8, 2, 256, 40960], P(('groups', 'ka'), None, None, 'pw'), parts along dimension 0, may hold values from -0.375 to 0.375
- shifts: int32 [8, 2, 40960], P(('groups', 'ka'), None, 'pw'), parts along dimension 0, may hold values from 0 to 40959, as said below
Outputs:
- correlations: float32 [8, 2, 2, 256, 256], P(('groups', 'ka')), parts along dimension 0
The draws below stay inside these ranges and needn't reach their ends.
There are 2 independent parts, one for each index of `groups`. The reference program is written for one: setup_inputs(seed, part) draws one part's arguments, and reference() takes and returns one part's arrays. A program takes and returns all parts, laid end to end along the dimension named above; each array names one. Nothing has to cross between parts.
Inputs may be any that keep to these rules, and one draw needn't show every extreme that they name: For every k, shifts[k, 0] maps each aligned block of 256 plane waves onto itself, one to one; shifts[k, 1] is the inverse permutation of shifts[(k - 1) mod 4, 0].
All inputs are finite; a program needn't handle non-finite values.
Results may differ from the reference program's by a relative error of at most 0.0003.
Values may be sent and summed in bfloat16 or wider, within the bound.
No kernel may reach another device: no remote copies, remote signals or barrier semaphores. Data moves between devices by JAX's collectives and lax.ppermute only.
A program may use at most 128 MiB of HBM per device.

```python
import jax
import jax.numpy as jnp
from jax import lax

NB = 256
NPW = 40960
PWB = 256
KX = 4


def draw_shifts(key, part):
    key = jax.random.fold_in(key, 11)
    blocks = NPW // PWB
    scores = jax.random.randint(key, (KX, blocks, PWB), 0, 1 << 20, dtype=jnp.int32)
    scores = scores * PWB + jnp.arange(PWB, dtype=jnp.int32)
    order = jnp.argsort(scores, axis=-1, stable=True).astype(jnp.int32)
    inverse_order = jnp.argsort(order, axis=-1, stable=True).astype(jnp.int32)
    offsets = (jnp.arange(blocks, dtype=jnp.int32) * PWB)[None, :, None]
    forward = (order + offsets).reshape(KX, NPW)
    backward = jnp.roll((inverse_order + offsets).reshape(KX, NPW), 1, axis=0)
    return jnp.stack([forward, backward], axis=1)


def steps_of(own_key, extent, shards, low, largest):
    loudness = 1.0
    for dim, parts in shards:
        steps = jax.random.uniform(jax.random.fold_in(jax.random.fold_in(own_key, 6), dim), (parts,), jnp.float32, low / len(shards), largest / len(shards))
        loudness = loudness * jnp.repeat(jnp.exp(steps), extent[dim] // parts).reshape((-1,) + (1,) * (len(extent) - 1 - dim))
    return loudness


def scatter_about(stream_key, shape, width, most, cuts=(), kind=jnp.bfloat16):
    drawn = width * jax.random.normal(stream_key, shape, jnp.float32)
    if cuts:
        drawn = drawn * steps_of(stream_key, shape, cuts, -0.22, 0.18)
    return jnp.clip(drawn, -most, most).astype(kind)


def setup_inputs(seed: int = 0, part: int = 0) -> dict:
    streams_of = jax.random.split(jax.random.key(seed), 3)
    part_splits = jax.random.split(jax.random.fold_in(streams_of[2], part), 3)
    coefficients = scatter_about(part_splits[0], (KX, 2, NB, NPW), ((2 * NPW) ** -0.25), 0.375, ((0, 4), (3, 4)))
    shifts = draw_shifts(jax.random.fold_in(jax.random.fold_in(streams_of[2], part), 71), part)
    return {"coefficients": coefficients, "shifts": shifts}


def correlation_of(own_bands, partner):
    bands = own_bands.shape[1]
    product = lax.dot_general(own_bands.reshape(2 * bands, -1), partner.reshape(2 * bands, -1), (((1,), (1,)), ((), ())), preferred_element_type=jnp.float32)
    real_part = product[:bands, :bands] + product[bands:, bands:]
    imag_part = product[:bands, bands:] - product[bands:, :bands]
    return jnp.stack([real_part, imag_part])


def reference(coefficients, shifts):
    def per_point(kpoint):
        own_bands = coefficients[kpoint]
        ahead_bands = jnp.take(coefficients[(kpoint + 1) % KX], shifts[kpoint, 0], axis=2)
        behind_bands = jnp.take(coefficients[(kpoint + KX - 1) % KX], shifts[kpoint, 1], axis=2)
        return jnp.stack([correlation_of(own_bands, ahead_bands), correlation_of(own_bands, behind_bands)])

    return lax.map(per_point, jnp.arange(KX, dtype=jnp.int32))
```

```python
import jax
import jax.numpy as jnp
from jax import lax
from jax.sharding import PartitionSpec as P

PWB = 256
SIXTEENTHS = (2, 4, 4, 3, 2, 1)
IN_FLIGHT = 2


def moved(block, axis, distance):
    count = lax.axis_size(axis)
    return lax.ppermute(block, axis, [(i, (i + distance) % count) for i in range(count)])


def moved_both(block, ka_distance, pw_distance):
    ka, pw = lax.axis_size("ka"), lax.axis_size("pw")
    route = [
        (k * pw + p, (k + ka_distance) % ka * pw + (p + pw_distance) % pw)
        for k in range(ka)
        for p in range(pw)
    ]
    return lax.ppermute(block, ("ka", "pw"), route)


def unpermuted(bands_block, table):
    width = bands_block.shape[2]
    block_count = width // PWB
    block_start = (jnp.arange(block_count, dtype=jnp.int32) * PWB)[:, None]
    inside = table.reshape(block_count, PWB) - block_start
    selector = (inside[:, :, None] == jnp.arange(PWB, dtype=jnp.int32)[None, None, :]).astype(
        jnp.bfloat16
    )
    rows = bands_block.reshape(-1, block_count, PWB)
    placed = jnp.einsum("rbo,boi->rbi", rows, selector, preferred_element_type=jnp.float32)
    return placed.astype(jnp.bfloat16).reshape(bands_block.shape)


def correlation_of(own, partner):
    bands = own.shape[1]
    some = partner.shape[1]
    product = lax.dot_general(
        own.reshape(2 * bands, -1),
        partner.reshape(2 * some, -1),
        (((1,), (1,)), ((), ())),
        preferred_element_type=jnp.float32,
    )
    real_part = product[:bands, :some] + product[bands:, some:]
    imag_part = product[:bands, some:] - product[bands:, :some]
    return jnp.stack([real_part, imag_part])


def mirrored(matrix):
    turned = jnp.swapaxes(matrix, -1, -2)
    return jnp.stack([turned[..., 0, :, :], -turned[..., 1, :, :]], axis=-3)


def summed_in_shares(partial):
    pw = lax.axis_size("pw")
    me = lax.axis_index("pw")
    bands, some = partial.shape[1:]
    rows = bands // pw
    share = lax.dynamic_slice_in_dim(partial, me * rows, rows, 1)
    for d in range(1, pw):
        piece = lax.dynamic_slice_in_dim(partial, lax.rem(me + d, pw) * rows, rows, 1)
        share = share + moved(piece, "pw", d)
    pair = jnp.stack([share, moved(share, "ka", 1)])
    whole = jnp.zeros((2, 2, bands, some), jnp.float32)
    whole = lax.dynamic_update_slice_in_dim(whole, pair, me * rows, 2)
    for d in range(1, pw):
        got = moved(pair, "pw", d)
        whole = lax.dynamic_update_slice_in_dim(whole, got, lax.rem(me + pw - d, pw) * rows, 2)
    return whole[0], whole[1]


def summed_at_once(partial):
    pw = lax.axis_size("pw")
    here = partial
    for d in range(1, pw):
        here = here + moved(partial, "pw", d)
    before = moved_both(partial, 1, 0)
    for d in range(1, pw):
        before = before + moved_both(partial, 1, d)
    return here, before


def local(coefficients, shifts):
    own = coefficients[0]
    bands, pw_width = own.shape[1:]
    table = shifts[0, 0] - lax.axis_index("pw") * pw_width
    unit = bands // sum(SIXTEENTHS)
    arrived = []
    start = 0
    for index, size in enumerate(SIXTEENTHS):
        block = own[:, start : start + size * unit]
        if index >= IN_FLIGHT:
            block, arrived[index - IN_FLIGHT] = lax.optimization_barrier(
                (block, arrived[index - IN_FLIGHT])
            )
        arrived.append(moved(block, "ka", -1))
        start += size * unit
    placed = unpermuted(own, table)
    partials = [correlation_of(placed, block) for block in arrived]
    most_ahead, most_behind = summed_in_shares(jnp.concatenate(partials[:-1], axis=2))
    last_ahead, last_behind = summed_at_once(partials[-1])
    ahead = jnp.concatenate([most_ahead, last_ahead], axis=2)
    behind = jnp.concatenate([mirrored(most_behind), mirrored(last_behind)], axis=1)
    return jnp.stack([ahead, behind])[None]


def solution(mesh):
    return jax.shard_map(
        local,
        mesh=mesh,
        in_specs=(P(("groups", "ka"), None, None, "pw"), P(("groups", "ka"), None, "pw")),
        out_specs=P(("groups", "ka"), None, None, None, None),
        check_vma=False,
    )
```

```python
import jax
import jax.numpy as jnp
from jax import lax
from jax.sharding import PartitionSpec as P

PWB = 256
SIXTEENTHS = (1, 3, 4, 4, 2, 1, 1)


def moved(block, axis, distance):
    count = lax.axis_size(axis)
    return lax.ppermute(block, axis, [(i, (i + distance) % count) for i in range(count)])


def after(value, *others):
    return lax.optimization_barrier((value, *others))[0]


def unpermuted(bands_block, table):
    width = bands_block.shape[2]
    block_count = width // PWB
    block_start = (jnp.arange(block_count, dtype=jnp.int32) * PWB)[:, None]
    inside = table.reshape(block_count, PWB) - block_start
    selector = (inside[:, :, None] == jnp.arange(PWB, dtype=jnp.int32)[None, None, :]).astype(
        jnp.bfloat16
    )
    rows = bands_block.reshape(-1, block_count, PWB)
    placed = jnp.einsum("rbo,boi->rbi", rows, selector, preferred_element_type=jnp.float32)
    return placed.astype(jnp.bfloat16).reshape(bands_block.shape)


def correlation_of(own, partner):
    bands = own.shape[1]
    some = partner.shape[1]
    product = lax.dot_general(
        own.reshape(2 * bands, -1),
        partner.reshape(2 * some, -1),
        (((1,), (1,)), ((), ())),
        preferred_element_type=jnp.float32,
    )
    real_part = product[:bands, :some] + product[bands:, some:]
    imag_part = product[:bands, some:] - product[bands:, :some]
    return jnp.stack([real_part, imag_part])


def mirrored(matrix):
    turned = jnp.swapaxes(matrix, -1, -2)
    return jnp.stack([turned[0], -turned[1]])


def exchanged(pieces):
    return lax.all_to_all(pieces, "pw", 0, 0, tiled=True)


def share_of_sum(partial):
    pw = lax.axis_size("pw")
    bands, some = partial.shape[1:]
    pieces = jnp.swapaxes(partial.reshape(2, pw, bands // pw, some), 0, 1)
    return jnp.sum(exchanged(pieces), axis=0)


def all_shares(pair):
    pw = lax.axis_size("pw")
    shares = exchanged(jnp.broadcast_to(pair[None], (pw, *pair.shape)))
    whole = jnp.moveaxis(shares, 0, 2)
    return whole.reshape(*pair.shape[:2], -1, pair.shape[3])


def whole_sum(partial):
    pw = lax.axis_size("pw")
    return jnp.sum(exchanged(jnp.broadcast_to(partial[None], (pw, *partial.shape))), axis=0)


def local(coefficients, shifts):
    own = coefficients[0]
    bands, pw_width = own.shape[1:]
    table = shifts[0, 0] - lax.axis_index("pw") * pw_width
    unit = bands // sum(SIXTEENTHS)
    edges = [0]
    for size in SIXTEENTHS:
        edges.append(edges[-1] + size * unit)

    def sent(chunk, *others):
        block = own[:, edges[chunk] : edges[chunk + 1]]
        return moved(after(block, *others) if others else block, "ka", -1)

    arrived = {0: sent(0)}
    arrived[1] = sent(1)
    arrived[2] = sent(2)
    placed = unpermuted(own, table)
    partial = {}

    def correlate(chunk, *others):
        block = arrived[chunk]
        partial[chunk] = correlation_of(placed, after(block, *others) if others else block)

    correlate(0)
    arrived[3] = sent(3, arrived[0])
    correlate(1, partial[0])
    arrived[4] = sent(4, arrived[1])
    correlate(2, partial[1])
    arrived[5] = sent(5, arrived[2])
    first = share_of_sum(jnp.concatenate([partial[0], partial[1], partial[2]], axis=2))
    first_behind = moved(first, "ka", 1)
    correlate(3, first)
    arrived[6] = sent(6, arrived[3])
    second = share_of_sum(partial[3])
    second_behind = moved(second, "ka", 1)
    first_whole = all_shares(jnp.stack([first, first_behind]))
    correlate(4, first_whole, second)
    third = whole_sum(partial[4])
    third_behind = moved(third, "ka", 1)
    second_whole = all_shares(jnp.stack([second, after(second_behind, third)]))
    correlate(5, second_whole, third)
    fourth = whole_sum(partial[5])
    fourth_behind = moved(fourth, "ka", 1)
    correlate(6, fourth)
    fifth = whole_sum(partial[6])
    fifth_behind = moved(fifth, "ka", 1)
    ahead = jnp.concatenate([first_whole[0], second_whole[0], third, fourth, fifth], axis=2)
    behind = jnp.concatenate(
        [
            mirrored(before)
            for before in (
                first_whole[1],
                second_whole[1],
                third_behind,
                fourth_behind,
                fifth_behind,
            )
        ],
        axis=1,
    )
    return jnp.stack([ahead, behind])[None]


def solution(mesh):
    return jax.shard_map(
        local,
        mesh=mesh,
        in_specs=(P(("groups", "ka"), None, None, "pw"), P(("groups", "ka"), None, "pw")),
        out_specs=P(("groups", "ka"), None, None, None, None),
        check_vma=False,
    )
```

```python
import functools

import jax
import jax.numpy as jnp
from jax import lax
from jax.experimental import pallas as pl
from jax.experimental.pallas import tpu as pltpu
from jax.sharding import PartitionSpec as P

PWB = 256
SIXTEENTHS = (5, 4, 3, 2, 1, 1)
MIB = 1 << 20
ANYWHERE = pl.BlockSpec(memory_space=pl.ANY)
WHOLE = pl.BlockSpec(memory_space=pltpu.VMEM)


def moved(block, axis, distance):
    count = lax.axis_size(axis)
    return lax.ppermute(block, axis, [(i, (i + distance) % count) for i in range(count)])


def cut_kernel(low, high, *refs):
    own_ref, out_ref, sems = refs[0], refs[-2], refs[-1]
    copies = [
        pltpu.make_async_copy(own_ref.at[0, c, low:high], out_ref.at[c], sems.at[c])
        for c in range(2)
    ]
    for copy in copies:
        copy.start()
    for copy in copies:
        copy.wait()


def cut(coefficients, low, high, *others):
    shape = (2, high - low, coefficients.shape[3])
    return pl.pallas_call(
        functools.partial(cut_kernel, low, high),
        out_shape=jax.ShapeDtypeStruct(shape, coefficients.dtype),
        in_specs=[ANYWHERE] * (1 + len(others)),
        out_specs=ANYWHERE,
        scratch_shapes=[pltpu.SemaphoreType.DMA((2,))],
        compiler_params=pltpu.CompilerParams(vmem_limit_bytes=MIB),
        cost_estimate=pl.CostEstimate(flops=0, bytes_accessed=1024, transcendentals=0),
        name="cut",
    )(coefficients, *others)


def place_kernel(own_ref, shift_ref, out_ref):
    bands, width = own_ref.shape[2:]
    base = pl.program_id(0) * width
    goal = lax.broadcasted_iota(jnp.int32, (PWB, PWB), 0)
    for block in range(width // PWB):
        here = pl.ds(block * PWB, PWB)
        inside = shift_ref[0, 0:1, here] & (PWB - 1)
        selector = (goal == inside).astype(jnp.float32).astype(jnp.bfloat16)
        rows = own_ref[0, :, :, here].reshape(2 * bands, PWB)
        placed = lax.dot_general(
            selector, rows, (((1,), (1,)), ((), ())), preferred_element_type=jnp.float32
        )
        there = pl.multiple_of(base + block * PWB, PWB)
        out_ref[pl.ds(there, PWB), :] = placed.astype(jnp.bfloat16)


def placed_bands(coefficients, shifts):
    bands, width = coefficients.shape[2:]
    step = 4 * PWB if width % (4 * PWB) == 0 else PWB
    return pl.pallas_call(
        place_kernel,
        grid=(width // step,),
        out_shape=pltpu.VMEM((width, 2 * bands), jnp.bfloat16),
        in_specs=[
            pl.BlockSpec((1, 2, bands, step), lambda g: (0, 0, 0, g)),
            pl.BlockSpec((1, 2, step), lambda g: (0, 0, g)),
        ],
        out_specs=WHOLE,
        compiler_params=pltpu.CompilerParams(vmem_limit_bytes=16 * MIB),
        cost_estimate=pl.CostEstimate(flops=0, bytes_accessed=1024, transcendentals=0),
        name="place",
    )(coefficients, shifts)


def correlate_kernel(steps, *refs):
    placed_ref, block_ref, out_ref, total = refs[0], refs[1], refs[-2], refs[-1]
    some, depth = block_ref.shape[1:]
    bands = out_ref.shape[2]
    step = pl.program_id(0)
    start = pl.multiple_of(step * depth, PWB)
    product = jnp.dot(
        block_ref[...].reshape(2 * some, depth),
        placed_ref[pl.ds(start, depth), :],
        preferred_element_type=jnp.float32,
    )

    @pl.when(step == 0)
    def _():
        total[...] = product

    @pl.when(step > 0)
    def _():
        total[...] += product

    @pl.when(step == steps - 1)
    def _():
        out_ref[0] = total[:some, :bands] + total[some:, bands:]
        out_ref[1] = total[some:, :bands] - total[:some, bands:]


def correlate(placed, block, *others):
    some, width = block.shape[1:]
    bands = placed.shape[1] // 2
    depth = width
    while depth % (2 * PWB) == 0 and some * depth > 1 << 18:
        depth //= 2
    steps = width // depth
    return pl.pallas_call(
        functools.partial(correlate_kernel, steps),
        grid=(steps,),
        out_shape=jax.ShapeDtypeStruct((2, some, bands), jnp.float32),
        in_specs=[WHOLE, pl.BlockSpec((2, some, depth), lambda g: (0, 0, g))]
        + [ANYWHERE] * len(others),
        out_specs=pl.BlockSpec((2, some, bands), lambda g: (0, 0, 0)),
        scratch_shapes=[pltpu.VMEM((2 * some, 2 * bands), jnp.float32)],
        compiler_params=pltpu.CompilerParams(vmem_limit_bytes=16 * MIB),
        cost_estimate=pl.CostEstimate(flops=0, bytes_accessed=1024, transcendentals=0),
        name="correlate",
    )(placed, block, *others)


def summed_over_pw(partial):
    pw = lax.axis_size("pw")
    if pw & (pw - 1):
        return partial + sum(moved(partial, "pw", d) for d in range(1, pw))
    distance = 1
    while distance < pw:
        route = [(i, i ^ distance) for i in range(pw)]
        partial = partial + lax.ppermute(partial, "pw", route)
        distance *= 2
    return partial


def local(coefficients, shifts):
    bands = coefficients.shape[2]
    unit = bands // sum(SIXTEENTHS)
    edges = [0]
    for size in SIXTEENTHS:
        edges.append(edges[-1] + size * unit)
    coefficients = pltpu.with_memory_space_constraint(coefficients, pltpu.HBM)
    placed = pltpu.with_memory_space_constraint(placed_bands(coefficients, shifts), pltpu.VMEM)
    blocks, arrived = [], []
    for chunk, (low, high) in enumerate(zip(edges, edges[1:])):
        before = blocks[-1:] + ([arrived[chunk - 3], placed] if chunk >= 3 else [])
        blocks.append(cut(coefficients, low, high, *before))
        arrived.append(moved(blocks[-1], "ka", -1))
    partial, whole = [], []
    for chunk, block in enumerate(arrived):
        before = partial[-1:] + whole[max(0, chunk - 1 - (chunk > 3)) : chunk - (chunk > 3)]
        partial.append(correlate(placed, block, *before))
        whole.append(summed_over_pw(partial[-1]))
    behind = [
        moved(jnp.concatenate(some, axis=1), "ka", 1)
        for some in (whole[:3], whole[3:5], whole[5:])
    ]
    ahead = jnp.swapaxes(jnp.concatenate(whole, axis=1), 1, 2)
    behind = jnp.concatenate(behind, axis=1)
    return jnp.stack([ahead, jnp.stack([behind[0], -behind[1]])])[None]


def solution(mesh):
    return jax.shard_map(
        local,
        mesh=mesh,
        in_specs=(P(("groups", "ka"), None, None, "pw"), P(("groups", "ka"), None, "pw")),
        out_specs=P(("groups", "ka"), None, None, None, None),
        check_vma=False,
    )
```

```python
import functools

import jax
import jax.numpy as jnp
from jax import lax
from jax.experimental import pallas as pl
from jax.experimental.pallas import tpu as pltpu
from jax.sharding import PartitionSpec as P

PWB = 256
SIXTEENTHS = (5, 4, 3, 2, 2)
MIB = 1 << 20
ANYWHERE = pl.BlockSpec(memory_space=pl.ANY)
WHOLE = pl.BlockSpec(memory_space=pltpu.VMEM)


def moved(block, axis, distance):
    count = lax.axis_size(axis)
    return lax.ppermute(block, axis, [(i, (i + distance) % count) for i in range(count)])


def cut_kernel(low, high, *refs):
    own_ref, out_ref, sems = refs[0], refs[-2], refs[-1]
    copies = [
        pltpu.make_async_copy(own_ref.at[0, c, low:high], out_ref.at[c], sems.at[c])
        for c in range(2)
    ]
    for copy in copies:
        copy.start()
    for copy in copies:
        copy.wait()


def cut(coefficients, low, high, *others):
    shape = (2, high - low, coefficients.shape[3])
    return pl.pallas_call(
        functools.partial(cut_kernel, low, high),
        out_shape=jax.ShapeDtypeStruct(shape, coefficients.dtype),
        in_specs=[ANYWHERE] * (1 + len(others)),
        out_specs=ANYWHERE,
        scratch_shapes=[pltpu.SemaphoreType.DMA((2,))],
        compiler_params=pltpu.CompilerParams(vmem_limit_bytes=MIB),
        cost_estimate=pl.CostEstimate(flops=0, bytes_accessed=1024, transcendentals=0),
        name="cut",
    )(coefficients, *others)


def place_kernel(own_ref, shift_ref, out_ref):
    bands, width = own_ref.shape[2:]
    base = pl.program_id(0) * width
    goal = lax.broadcasted_iota(jnp.int32, (PWB, PWB), 0)
    for block in range(width // PWB):
        here = pl.ds(block * PWB, PWB)
        inside = shift_ref[0, 0:1, here] & (PWB - 1)
        selector = (goal == inside).astype(jnp.float32).astype(jnp.bfloat16)
        rows = own_ref[0, :, :, here].reshape(2 * bands, PWB)
        placed = lax.dot_general(
            selector, rows, (((1,), (1,)), ((), ())), preferred_element_type=jnp.float32
        )
        there = pl.multiple_of(base + block * PWB, PWB)
        out_ref[pl.ds(there, PWB), :] = placed.astype(jnp.bfloat16)


def placed_bands(coefficients, shifts):
    bands, width = coefficients.shape[2:]
    step = 4 * PWB if width % (4 * PWB) == 0 else PWB
    return pl.pallas_call(
        place_kernel,
        grid=(width // step,),
        out_shape=pltpu.VMEM((width, 2 * bands), jnp.bfloat16),
        in_specs=[
            pl.BlockSpec((1, 2, bands, step), lambda g: (0, 0, 0, g)),
            pl.BlockSpec((1, 2, step), lambda g: (0, 0, g)),
        ],
        out_specs=WHOLE,
        compiler_params=pltpu.CompilerParams(vmem_limit_bytes=16 * MIB),
        cost_estimate=pl.CostEstimate(flops=0, bytes_accessed=1024, transcendentals=0),
        name="place",
    )(coefficients, shifts)


def correlate_kernel(out_at, depth, placed_ref, block_ref, *refs):
    out_ref, total = refs[out_at], refs[-1]
    some, width = block_ref.shape[1:]
    bands = out_ref.shape[2]

    def product_of(start):
        return jnp.dot(
            block_ref[:, :, pl.ds(start, depth)].reshape(2 * some, depth),
            placed_ref[pl.ds(start, depth), :],
            preferred_element_type=jnp.float32,
        )

    total[...] = product_of(0)

    @pl.loop(1, width // depth)
    def _(step):
        total[...] += product_of(pl.multiple_of(step * depth, depth))

    out_ref[0] = total[:some, :bands] + total[some:, bands:]
    out_ref[1] = total[some:, :bands] - total[:some, bands:]


def correlate(placed, block, *others, held=None):
    some, width = block.shape[1:]
    bands = placed.shape[1] // 2
    depth = width
    while depth % (2 * PWB) == 0 and some * depth > 1 << 19:
        depth //= 2
    block = pltpu.with_memory_space_constraint(block, pltpu.VMEM)
    out_shape = [jax.ShapeDtypeStruct((2, some, bands), jnp.float32)]
    aliases = {}
    if held is not None:
        others = (*others, held)
        aliases = {1 + len(others): 1}
        out_shape.append(jax.ShapeDtypeStruct(held.shape, held.dtype))
    out = pl.pallas_call(
        functools.partial(correlate_kernel, len(others), depth),
        out_shape=out_shape,
        in_specs=[WHOLE, WHOLE] + [ANYWHERE] * len(others),
        out_specs=[WHOLE, ANYWHERE][: len(out_shape)],
        scratch_shapes=[pltpu.VMEM((2 * some, 2 * bands), jnp.float32)],
        input_output_aliases=aliases,
        compiler_params=pltpu.CompilerParams(vmem_limit_bytes=16 * MIB),
        cost_estimate=pl.CostEstimate(flops=0, bytes_accessed=1024, transcendentals=0),
        name="correlate",
    )(placed, block, *others)
    return out[0] if held is None else out


def summed_over_pw(partial):
    pw = lax.axis_size("pw")
    if pw & (pw - 1):
        return partial + sum(moved(partial, "pw", d) for d in range(1, pw))
    distance = 1
    while distance < pw:
        partial = partial + lax.ppermute(partial, "pw", [(i, i ^ distance) for i in range(pw)])
        distance *= 2
    return partial


def sums_here_and_next(partial):
    ka, pw = lax.axis_size("ka"), lax.axis_size("pw")
    if pw & (pw - 1) or pw == 1:
        whole = summed_over_pw(partial)
        return [whole], [moved(whole, "ka", 1)]
    distance = 1
    while 2 * distance < pw:
        partial = partial + lax.ppermute(partial, "pw", [(i, i ^ distance) for i in range(pw)])
        distance *= 2
    here = lax.ppermute(partial, "pw", [(i, i ^ distance) for i in range(pw)])
    across = [
        (k * pw + p, (k + 1) % ka * pw + (p ^ distance)) for k in range(ka) for p in range(pw)
    ]
    before = [moved(partial, "ka", 1), lax.ppermute(partial, ("ka", "pw"), across)]
    return [partial, here], before


def assemble_kernel(ahead_count, *refs):
    ins, (out_ref, made, sems) = refs[:-3], refs[-3:]
    most_ref, most_before_ref = ins[:2]
    last_refs = ins[2 : 2 + ahead_count], ins[2 + ahead_count :]
    copies = []
    for side in (1, 0):
        for c in (0, 1):
            early = (most_ref, most_before_ref)[side][c]
            late = sum(ref[c] for ref in last_refs[side])
            matrix = jnp.concatenate([early, late], axis=0)
            if side == 0:
                matrix = matrix.T
            elif c == 1:
                matrix = -matrix
            made[2 * side + c] = matrix
            copies.append(
                pltpu.make_async_copy(
                    made.at[2 * side + c], out_ref.at[0, side, c], sems.at[2 * side + c]
                )
            )
            copies[-1].start()
    for copy in copies:
        copy.wait()


def assembled(most, most_before, last, last_before):
    bands = most.shape[2]
    count = 2 + len(last) + len(last_before)
    return pl.pallas_call(
        functools.partial(assemble_kernel, len(last)),
        out_shape=jax.ShapeDtypeStruct((1, 2, 2, bands, bands), jnp.float32),
        in_specs=[WHOLE] * count,
        out_specs=ANYWHERE,
        scratch_shapes=[
            pltpu.VMEM((4, bands, bands), jnp.float32),
            pltpu.SemaphoreType.DMA((4,)),
        ],
        compiler_params=pltpu.CompilerParams(vmem_limit_bytes=16 * MIB),
        cost_estimate=pl.CostEstimate(flops=0, bytes_accessed=1024, transcendentals=0),
        name="assemble",
    )(most, most_before, *last, *last_before)


def local(coefficients, shifts):
    bands = coefficients.shape[2]
    unit = bands // sum(SIXTEENTHS)
    edges = [0]
    for size in SIXTEENTHS:
        edges.append(edges[-1] + size * unit)
    coefficients = pltpu.with_memory_space_constraint(coefficients, pltpu.HBM)
    placed = pltpu.with_memory_space_constraint(placed_bands(coefficients, shifts), pltpu.VMEM)
    blocks, arrived, whole = [], [], []

    def send(chunk, *others):
        blocks.append(
            cut(coefficients, edges[chunk], edges[chunk + 1], *blocks[-1:], *others)
        )
        arrived.append(moved(blocks[-1], "ka", -1))

    for chunk in range(3):
        send(chunk)
    send(3, arrived[0], placed)
    for chunk in range(4):
        if chunk == 1:
            send(4, arrived[1], whole[0])
        whole.append(summed_over_pw(correlate(placed, arrived[chunk], *whole[-1:])))
    most = jnp.concatenate(whole, axis=1)
    last, most = correlate(placed, arrived[-1], held=most)
    most_before = moved(most, "ka", 1)
    return assembled(most, most_before, *sums_here_and_next(last))


def solution(mesh):
    return jax.shard_map(
        local,
        mesh=mesh,
        in_specs=(P(("groups", "ka"), None, None, "pw"), P(("groups", "ka"), None, "pw")),
        out_specs=P(("groups", "ka"), None, None, None, None),
        check_vma=False,
    )
```

```python
import functools

import jax
import jax.numpy as jnp
from jax import lax
from jax.experimental import pallas as pl
from jax.experimental.pallas import tpu as pltpu
from jax.sharding import PartitionSpec as P

PWB = 256
SIXTEENTHS = (5, 4, 3, 2, 2)
MIB = 1 << 20
ANYWHERE = pl.BlockSpec(memory_space=pl.ANY)
WHOLE = pl.BlockSpec(memory_space=pltpu.VMEM)


def moved(block, axis, distance):
    count = lax.axis_size(axis)
    return lax.ppermute(block, axis, [(i, (i + distance) % count) for i in range(count)])


def cut_kernel(bands, waves, *refs):
    own_ref, out_ref, sems = refs[0], refs[-2], refs[-1]
    copies = [
        pltpu.make_async_copy(own_ref.at[0, c, bands, waves], out_ref.at[c], sems.at[c])
        for c in range(2)
    ]
    for copy in copies:
        copy.start()
    for copy in copies:
        copy.wait()


def cut(coefficients, bands, waves, *others):
    shape = (2, bands.stop - bands.start, waves.stop - waves.start)
    return pl.pallas_call(
        functools.partial(cut_kernel, bands, waves),
        out_shape=jax.ShapeDtypeStruct(shape, coefficients.dtype),
        in_specs=[ANYWHERE] * (1 + len(others)),
        out_specs=ANYWHERE,
        scratch_shapes=[pltpu.SemaphoreType.DMA((2,))],
        compiler_params=pltpu.CompilerParams(vmem_limit_bytes=MIB),
        cost_estimate=pl.CostEstimate(flops=0, bytes_accessed=1024, transcendentals=0),
        name="cut",
    )(coefficients, *others)


def place_kernel(own_ref, shift_ref, out_ref):
    bands, width = own_ref.shape[2:]
    base = pl.program_id(0) * width
    goal = lax.broadcasted_iota(jnp.int32, (PWB, PWB), 0)
    for block in range(width // PWB):
        here = pl.ds(block * PWB, PWB)
        inside = shift_ref[0, 0:1, here] & (PWB - 1)
        selector = (goal == inside).astype(jnp.float32).astype(jnp.bfloat16)
        rows = own_ref[0, :, :, here].reshape(2 * bands, PWB)
        placed = lax.dot_general(
            selector, rows, (((1,), (1,)), ((), ())), preferred_element_type=jnp.float32
        )
        there = pl.multiple_of(base + block * PWB, PWB)
        out_ref[pl.ds(there, PWB), :] = placed.astype(jnp.bfloat16)


def placed_bands(coefficients, shifts):
    bands, width = coefficients.shape[2:]
    step = 4 * PWB if width % (4 * PWB) == 0 else PWB
    return pl.pallas_call(
        place_kernel,
        grid=(width // step,),
        out_shape=pltpu.VMEM((width, 2 * bands), jnp.bfloat16),
        in_specs=[
            pl.BlockSpec((1, 2, bands, step), lambda g: (0, 0, 0, g)),
            pl.BlockSpec((1, 2, step), lambda g: (0, 0, g)),
        ],
        out_specs=WHOLE,
        compiler_params=pltpu.CompilerParams(vmem_limit_bytes=16 * MIB),
        cost_estimate=pl.CostEstimate(flops=0, bytes_accessed=1024, transcendentals=0),
        name="place",
    )(coefficients, shifts)


def correlate_kernel(first, depth, begun, held, placed_ref, block_ref, *refs):
    out_ref, total = refs[-2 - held], refs[-1]
    some, width = block_ref.shape[1:]
    bands = out_ref.shape[2]

    def product_of(start):
        return jnp.dot(
            block_ref[:, :, pl.ds(start, depth)].reshape(2 * some, depth),
            placed_ref[pl.ds(first + start, depth), :],
            preferred_element_type=jnp.float32,
        )

    total[...] = product_of(0)

    @pl.loop(1, width // depth)
    def _(step):
        total[...] += product_of(pl.multiple_of(step * depth, depth))

    real_part = total[:some, :bands] + total[some:, bands:]
    imag_part = total[some:, :bands] - total[:some, bands:]
    out_ref[0] = refs[0][0] + real_part if begun else real_part
    out_ref[1] = refs[0][1] + imag_part if begun else imag_part


def correlate(placed, block, *others, first=0, begun=None, held=()):
    some, width = block.shape[1:]
    bands = placed.shape[1] // 2
    depth = width
    while depth % (2 * PWB) == 0 and some * depth > 1 << 19:
        depth //= 2
    block = pltpu.with_memory_space_constraint(block, pltpu.VMEM)
    ins = [placed, block] if begun is None else [placed, block, begun]
    in_specs = [WHOLE] * len(ins) + [ANYWHERE] * (len(others) + len(held))
    before = len(ins) + len(others)
    product = jax.ShapeDtypeStruct((2, some, bands), jnp.float32)
    out = pl.pallas_call(
        functools.partial(correlate_kernel, first, depth, begun is not None, len(held)),
        out_shape=[product] + [jax.ShapeDtypeStruct(kept.shape, kept.dtype) for kept in held],
        in_specs=in_specs,
        out_specs=[WHOLE] + [ANYWHERE] * len(held),
        scratch_shapes=[pltpu.VMEM((2 * some, 2 * bands), jnp.float32)],
        input_output_aliases={before + index: 1 + index for index in range(len(held))},
        compiler_params=pltpu.CompilerParams(vmem_limit_bytes=16 * MIB),
        cost_estimate=pl.CostEstimate(flops=0, bytes_accessed=1024, transcendentals=0),
        name="correlate",
    )(*ins, *others, *held)
    return out if held else out[0]


def summed_over_pw(partial):
    pw = lax.axis_size("pw")
    if pw & (pw - 1):
        return partial + sum(moved(partial, "pw", d) for d in range(1, pw))
    distance = pw // 2
    while distance:
        partial = partial + lax.ppermute(partial, "pw", [(i, i ^ distance) for i in range(pw)])
        distance //= 2
    return partial


def sums_here_and_next(partial):
    ka, pw = lax.axis_size("ka"), lax.axis_size("pw")
    if pw & (pw - 1) or pw == 1:
        whole = summed_over_pw(partial)
        return [whole], [moved(whole, "ka", 1)]
    distance = pw // 2
    while distance > 1:
        partial = partial + lax.ppermute(partial, "pw", [(i, i ^ distance) for i in range(pw)])
        distance //= 2
    here = lax.ppermute(partial, "pw", [(i, i ^ 1) for i in range(pw)])
    across = [(k * pw + p, (k + 1) % ka * pw + (p ^ 1)) for k in range(ka) for p in range(pw)]
    before = [moved(partial, "ka", 1), lax.ppermute(partial, ("ka", "pw"), across)]
    return [partial, here], before


def assemble_kernel(counts, *refs):
    ins, (out_ref, made, sems) = list(refs[:-3]), refs[-3:]
    most, most_before, *last_refs = [[ins.pop(0) for _ in range(count)] for count in counts]
    copies = []
    for side in (1, 0):
        for c in (0, 1):
            early = [ref[c] for ref in (most, most_before)[side]]
            late = sum(ref[c] for ref in last_refs[side])
            matrix = jnp.concatenate([*early, late], axis=0)
            if side == 0:
                matrix = matrix.T
            elif c == 1:
                matrix = -matrix
            made[2 * side + c] = matrix
            copies.append(
                pltpu.make_async_copy(
                    made.at[2 * side + c], out_ref.at[0, side, c], sems.at[2 * side + c]
                )
            )
            copies[-1].start()
    for copy in copies:
        copy.wait()


def assembled(*parts):
    bands = parts[0][0].shape[2]
    counts = [len(part) for part in parts]
    return pl.pallas_call(
        functools.partial(assemble_kernel, counts),
        out_shape=jax.ShapeDtypeStruct((1, 2, 2, bands, bands), jnp.float32),
        in_specs=[WHOLE] * sum(counts),
        out_specs=ANYWHERE,
        scratch_shapes=[
            pltpu.VMEM((4, bands, bands), jnp.float32),
            pltpu.SemaphoreType.DMA((4,)),
        ],
        compiler_params=pltpu.CompilerParams(vmem_limit_bytes=16 * MIB),
        cost_estimate=pl.CostEstimate(flops=0, bytes_accessed=1024, transcendentals=0),
        name="assemble",
    )(*[array for part in parts for array in part])


def local(coefficients, shifts):
    bands, width = coefficients.shape[2:]
    unit = bands // sum(SIXTEENTHS)
    edges = [0]
    for size in SIXTEENTHS:
        edges.append(edges[-1] + size * unit)
    late = width // PWB * 3 // 4 * PWB
    coefficients = pltpu.with_memory_space_constraint(coefficients, pltpu.HBM)
    placed = pltpu.with_memory_space_constraint(placed_bands(coefficients, shifts), pltpu.VMEM)
    blocks, arrived, whole = [], [], []

    def send(chunk, low, high, *others):
        some = slice(edges[chunk], edges[chunk + 1])
        blocks.append(cut(coefficients, some, slice(low, high), *blocks[-1:], *others))
        arrived.append(moved(blocks[-1], "ka", -1))

    for chunk in range(3):
        send(chunk, 0, width)
    send(3, 0, width, arrived[0], placed)
    for chunk in range(4):
        if chunk == 1:
            send(4, 0, late, arrived[1], whole[0])
        if chunk == 2:
            send(4, late, width, arrived[2], whole[1])
        whole.append(summed_over_pw(correlate(placed, arrived[chunk], *whole[-1:])))
    halves = [jnp.concatenate(whole[:2], axis=1), jnp.concatenate(whole[2:], axis=1)]
    last = correlate(placed, arrived[4], *halves)
    last, *halves = correlate(placed, arrived[5], first=late, begun=last, held=halves)
    halves_before = [moved(half, "ka", 1) for half in halves]
    return assembled(halves, halves_before, *sums_here_and_next(last))


def solution(mesh):
    return jax.shard_map(
        local,
        mesh=mesh,
        in_specs=(P(("groups", "ka"), None, None, "pw"), P(("groups", "ka"), None, "pw")),
        out_specs=P(("groups", "ka"), None, None, None, None),
        check_vma=False,
    )
```

```python
import functools

import jax
import jax.numpy as jnp
from jax import lax
from jax.experimental import pallas as pl
from jax.experimental.pallas import tpu as pltpu
from jax.sharding import PartitionSpec as P

PWB = 256
SIXTEENTHS = (6, 4, 4, 2)
EVEN, ODD = 0, 1
MIB = 1 << 20
ANYWHERE = pl.BlockSpec(memory_space=pl.ANY)
WHOLE = pl.BlockSpec(memory_space=pltpu.VMEM)


def sent(block, kind, points=0, waves=0):
    ka, pw = lax.axis_size("ka"), lax.axis_size("pw")
    route = [
        (k * pw + p, (k + points) % ka * pw + (p ^ waves))
        for k in range(ka)
        for p in range(pw)
        if k % 2 == kind
    ]
    return lax.ppermute(block, ("ka", "pw"), route)


def fetched(block, kind):
    ka, pw = lax.axis_size("ka"), lax.axis_size("pw")
    route = [
        ((k + 1) % ka * pw + p, k * pw + p) for k in range(ka) for p in range(pw) if k % 2 == kind
    ]
    return lax.ppermute(block, ("ka", "pw"), route)


def cut_kernel(bands, waves, *refs):
    own_ref, out_ref, sems = refs[0], refs[-2], refs[-1]
    copies = [
        pltpu.make_async_copy(own_ref.at[0, c, bands, waves], out_ref.at[c], sems.at[c])
        for c in range(2)
    ]
    for copy in copies:
        copy.start()
    for copy in copies:
        copy.wait()


def cut(coefficients, bands, waves, *others):
    shape = (2, bands.stop - bands.start, waves.stop - waves.start)
    return pl.pallas_call(
        functools.partial(cut_kernel, bands, waves),
        out_shape=jax.ShapeDtypeStruct(shape, coefficients.dtype),
        in_specs=[ANYWHERE] * (1 + len(others)),
        out_specs=ANYWHERE,
        scratch_shapes=[pltpu.SemaphoreType.DMA((2,))],
        compiler_params=pltpu.CompilerParams(vmem_limit_bytes=MIB),
        cost_estimate=pl.CostEstimate(flops=0, bytes_accessed=1024, transcendentals=0),
        name="cut",
    )(coefficients, *others)


def place_kernel(own_ref, shift_ref, out_ref):
    bands, width = own_ref.shape[2:]
    base = pl.program_id(0) * width
    goal = lax.broadcasted_iota(jnp.int32, (PWB, PWB), 0)
    for block in range(width // PWB):
        here = pl.ds(block * PWB, PWB)
        inside = shift_ref[0, 0:1, here] & (PWB - 1)
        selector = (goal == inside).astype(jnp.float32).astype(jnp.bfloat16)
        rows = own_ref[0, :, :, here].reshape(2 * bands, PWB)
        placed = lax.dot_general(
            selector, rows, (((1,), (1,)), ((), ())), preferred_element_type=jnp.float32
        )
        there = pl.multiple_of(base + block * PWB, PWB)
        out_ref[pl.ds(there, PWB), :] = placed.astype(jnp.bfloat16)


def placed_bands(coefficients, shifts):
    bands, width = coefficients.shape[2:]
    step = 4 * PWB if width % (4 * PWB) == 0 else PWB
    return pl.pallas_call(
        place_kernel,
        grid=(width // step,),
        out_shape=pltpu.VMEM((width, 2 * bands), jnp.bfloat16),
        in_specs=[
            pl.BlockSpec((1, 2, bands, step), lambda g: (0, 0, 0, g)),
            pl.BlockSpec((1, 2, step), lambda g: (0, 0, g)),
        ],
        out_specs=WHOLE,
        compiler_params=pltpu.CompilerParams(vmem_limit_bytes=16 * MIB),
        cost_estimate=pl.CostEstimate(flops=0, bytes_accessed=1024, transcendentals=0),
        name="place",
    )(coefficients, shifts)


def correlate_kernel(first, depth, begun, held, placed_ref, block_ref, *refs):
    out_ref, total = refs[-2 - held], refs[-1]
    some, width = block_ref.shape[1:]
    bands = out_ref.shape[2]

    def product_of(start):
        return jnp.dot(
            block_ref[:, :, pl.ds(start, depth)].reshape(2 * some, depth),
            placed_ref[pl.ds(first + start, depth), :],
            preferred_element_type=jnp.float32,
        )

    total[...] = product_of(0)

    @pl.loop(1, width // depth)
    def _(step):
        total[...] += product_of(pl.multiple_of(step * depth, depth))

    real_part = total[:some, :bands] + total[some:, bands:]
    imag_part = total[some:, :bands] - total[:some, bands:]
    out_ref[0] = refs[0][0] + real_part if begun else real_part
    out_ref[1] = refs[0][1] + imag_part if begun else imag_part


def correlate(placed, block, *others, first=0, begun=None, held=()):
    some, width = block.shape[1:]
    bands = placed.shape[1] // 2
    depth = width
    while depth % (2 * PWB) == 0 and some * depth > 1 << 19:
        depth //= 2
    block = pltpu.with_memory_space_constraint(block, pltpu.VMEM)
    ins = [placed, block] if begun is None else [placed, block, begun]
    in_specs = [WHOLE] * len(ins) + [ANYWHERE] * (len(others) + len(held))
    before = len(ins) + len(others)
    product = jax.ShapeDtypeStruct((2, some, bands), jnp.float32)
    out = pl.pallas_call(
        functools.partial(correlate_kernel, first, depth, begun is not None, len(held)),
        out_shape=[product] + [jax.ShapeDtypeStruct(kept.shape, kept.dtype) for kept in held],
        in_specs=in_specs,
        out_specs=[WHOLE] + [ANYWHERE] * len(held),
        scratch_shapes=[pltpu.VMEM((2 * some, 2 * bands), jnp.float32)],
        input_output_aliases={before + index: 1 + index for index in range(len(held))},
        compiler_params=pltpu.CompilerParams(vmem_limit_bytes=16 * MIB),
        cost_estimate=pl.CostEstimate(flops=0, bytes_accessed=1024, transcendentals=0),
        name="correlate",
    )(*ins, *others, *held)
    return out if held else out[0]


def summed_over_pw(partial, kind, nearest=1):
    distance = lax.axis_size("pw") // 2
    while distance >= nearest:
        partial = partial + sent(partial, kind, waves=distance)
        distance //= 2
    return partial


def assemble_kernel(counts, *refs):
    ins, (out_ref, made, sems) = list(refs[:-3]), refs[-3:]
    parts = [[ins.pop(0) for _ in range(count)] for count in counts]
    copies = []
    for side in (1, 0):
        near, early, late = parts[3 * side : 3 * side + 3]
        for c in (0, 1):
            far = jnp.concatenate([ref[c] for ref in early] + [sum(ref[c] for ref in late)], axis=0)
            matrix = near[0][c] + far
            if side == 0:
                matrix = matrix.T
            elif c == 1:
                matrix = -matrix
            made[2 * side + c] = matrix
            copies.append(
                pltpu.make_async_copy(
                    made.at[2 * side + c], out_ref.at[0, side, c], sems.at[2 * side + c]
                )
            )
            copies[-1].start()
    for copy in copies:
        copy.wait()


def assembled(*parts):
    bands = parts[0][0].shape[2]
    counts = [len(part) for part in parts]
    return pl.pallas_call(
        functools.partial(assemble_kernel, counts),
        out_shape=jax.ShapeDtypeStruct((1, 2, 2, bands, bands), jnp.float32),
        in_specs=[WHOLE] * sum(counts),
        out_specs=ANYWHERE,
        scratch_shapes=[
            pltpu.VMEM((4, bands, bands), jnp.float32),
            pltpu.SemaphoreType.DMA((4,)),
        ],
        compiler_params=pltpu.CompilerParams(vmem_limit_bytes=16 * MIB),
        cost_estimate=pl.CostEstimate(flops=0, bytes_accessed=1024, transcendentals=0),
        name="assemble",
    )(*[array for part in parts for array in part])


def local(coefficients, shifts):
    bands, width = coefficients.shape[2:]
    unit = bands // sum(SIXTEENTHS)
    edges = [0]
    for size in SIXTEENTHS:
        edges.append(edges[-1] + size * unit)
    late = width // PWB * 3 // 4 * PWB
    near_block = fetched(coefficients[0], EVEN)
    coefficients = pltpu.with_memory_space_constraint(coefficients, pltpu.HBM)
    placed = pltpu.with_memory_space_constraint(placed_bands(coefficients, shifts), pltpu.VMEM)
    blocks, arrived, whole = [], [], []

    def send(chunk, low, high, *others):
        some = slice(edges[chunk], edges[chunk + 1])
        blocks.append(cut(coefficients, some, slice(low, high), *blocks[-1:], *others))
        arrived.append(fetched(blocks[-1], ODD))

    for chunk in range(3):
        send(chunk, 0, width)
    near = summed_over_pw(correlate(placed, near_block), EVEN)
    near_before = sent(near, EVEN, points=1)
    send(3, 0, late, arrived[0], placed)
    for chunk in range(3):
        if chunk == 2:
            send(3, late, width, arrived[1], whole[0])
        before = whole[-1] if whole else near
        whole.append(summed_over_pw(correlate(placed, arrived[chunk], before), ODD))
    halves = [jnp.concatenate(whole[:2], axis=1), whole[2]]
    last = correlate(placed, arrived[3], *halves)
    last, *halves = correlate(placed, arrived[4], first=late, begun=last, held=halves)
    halves_before = [sent(half, ODD, points=1) for half in halves]
    last = summed_over_pw(last, ODD, nearest=2)
    ahead = [last, sent(last, ODD, waves=1)]
    behind = [sent(last, ODD, points=1), sent(last, ODD, points=1, waves=1)]
    return assembled([near], halves, ahead, [near_before], halves_before, behind)


def solution(mesh):
    return jax.shard_map(
        local,
        mesh=mesh,
        in_specs=(P(("groups", "ka"), None, None, "pw"), P(("groups", "ka"), None, "pw")),
        out_specs=P(("groups", "ka"), None, None, None, None),
        check_vma=False,
    )
```

```python
import functools

import jax
import jax.numpy as jnp
from jax import lax
from jax.experimental import pallas as pl
from jax.experimental.pallas import tpu as pltpu
from jax.sharding import PartitionSpec as P

PWB = 256
SIXTEENTHS = (6, 4, 2, 2, 2)
EVEN, ODD, ALL = (0,), (1,), (0, 1)
MIB = 1 << 20
ANYWHERE = pl.BlockSpec(memory_space=pl.ANY)
WHOLE = pl.BlockSpec(memory_space=pltpu.VMEM)


def routed(block, goal):
    ka, pw = lax.axis_size("ka"), lax.axis_size("pw")
    route = []
    for k in range(ka):
        for p in range(pw):
            point, share = goal(k, p)
            route.append((k * pw + p, point % ka * pw + share))
    return lax.ppermute(block, ("ka", "pw"), route)


def fetched(block):
    return routed(block, lambda k, p: (k - 1, p))


def swapped(block):
    return routed(block, lambda k, p: (k ^ 1, p))


def exchanged(block, kinds, distance):
    return routed(block, lambda k, p: (k, p ^ distance if k % 2 in kinds else p))


def cut_kernel(bands, waves, *refs):
    own_ref, out_ref, sems = refs[0], refs[-2], refs[-1]
    copies = [
        pltpu.make_async_copy(own_ref.at[0, c, bands, waves], out_ref.at[c], sems.at[c])
        for c in range(2)
    ]
    for copy in copies:
        copy.start()
    for copy in copies:
        copy.wait()


def cut(coefficients, bands, waves, *others):
    shape = (2, bands.stop - bands.start, waves.stop - waves.start)
    return pl.pallas_call(
        functools.partial(cut_kernel, bands, waves),
        out_shape=jax.ShapeDtypeStruct(shape, coefficients.dtype),
        in_specs=[ANYWHERE] * (1 + len(others)),
        out_specs=ANYWHERE,
        scratch_shapes=[pltpu.SemaphoreType.DMA((2,))],
        compiler_params=pltpu.CompilerParams(vmem_limit_bytes=MIB),
        cost_estimate=pl.CostEstimate(flops=0, bytes_accessed=1024, transcendentals=0),
        name="cut",
    )(coefficients, *others)


def place_kernel(own_ref, shift_ref, out_ref):
    bands, width = own_ref.shape[2:]
    base = pl.program_id(0) * width
    goal = lax.broadcasted_iota(jnp.int32, (PWB, PWB), 0)
    for block in range(width // PWB):
        here = pl.ds(block * PWB, PWB)
        inside = shift_ref[0, 0:1, here] & (PWB - 1)
        selector = (goal == inside).astype(jnp.float32).astype(jnp.bfloat16)
        rows = own_ref[0, :, :, here].reshape(2 * bands, PWB)
        placed = lax.dot_general(
            selector, rows, (((1,), (1,)), ((), ())), preferred_element_type=jnp.float32
        )
        there = pl.multiple_of(base + block * PWB, PWB)
        out_ref[pl.ds(there, PWB), :] = placed.astype(jnp.bfloat16)


def placed_bands(coefficients, shifts):
    bands, width = coefficients.shape[2:]
    step = 4 * PWB if width % (4 * PWB) == 0 else PWB
    return pl.pallas_call(
        place_kernel,
        grid=(width // step,),
        out_shape=pltpu.VMEM((width, 2 * bands), jnp.bfloat16),
        in_specs=[
            pl.BlockSpec((1, 2, bands, step), lambda g: (0, 0, 0, g)),
            pl.BlockSpec((1, 2, step), lambda g: (0, 0, g)),
        ],
        out_specs=WHOLE,
        compiler_params=pltpu.CompilerParams(vmem_limit_bytes=16 * MIB),
        cost_estimate=pl.CostEstimate(flops=0, bytes_accessed=1024, transcendentals=0),
        name="place",
    )(coefficients, shifts)


def correlate_kernel(first, depth, begun, held, placed_ref, block_ref, *refs):
    out_ref, total = refs[-2 - held], refs[-1]
    some, width = block_ref.shape[1:]
    bands = out_ref.shape[2]

    def product_of(start):
        return jnp.dot(
            block_ref[:, :, pl.ds(start, depth)].reshape(2 * some, depth),
            placed_ref[pl.ds(first + start, depth), :],
            preferred_element_type=jnp.float32,
        )

    total[...] = product_of(0)

    @pl.loop(1, width // depth)
    def _(step):
        total[...] += product_of(pl.multiple_of(step * depth, depth))

    real_part = total[:some, :bands] + total[some:, bands:]
    imag_part = total[some:, :bands] - total[:some, bands:]
    out_ref[0] = refs[0][0] + real_part if begun else real_part
    out_ref[1] = refs[0][1] + imag_part if begun else imag_part


def correlate(placed, block, *others, first=0, begun=None, held=()):
    some, width = block.shape[1:]
    bands = placed.shape[1] // 2
    depth = width
    while depth % (2 * PWB) == 0 and some * depth > 1 << 19:
        depth //= 2
    block = pltpu.with_memory_space_constraint(block, pltpu.VMEM)
    ins = [placed, block] if begun is None else [placed, block, begun]
    in_specs = [WHOLE] * len(ins) + [ANYWHERE] * (len(others) + len(held))
    before = len(ins) + len(others)
    product = jax.ShapeDtypeStruct((2, some, bands), jnp.float32)
    out = pl.pallas_call(
        functools.partial(correlate_kernel, first, depth, begun is not None, len(held)),
        out_shape=[product] + [jax.ShapeDtypeStruct(kept.shape, kept.dtype) for kept in held],
        in_specs=in_specs,
        out_specs=[WHOLE] + [ANYWHERE] * len(held),
        scratch_shapes=[pltpu.VMEM((2 * some, 2 * bands), jnp.float32)],
        input_output_aliases={before + index: 1 + index for index in range(len(held))},
        compiler_params=pltpu.CompilerParams(vmem_limit_bytes=16 * MIB),
        cost_estimate=pl.CostEstimate(flops=0, bytes_accessed=1024, transcendentals=0),
        name="correlate",
    )(*ins, *others, *held)
    return out if held else out[0]


def summed_over_pw(partial, kinds, nearest=1):
    distance = lax.axis_size("pw") // 2
    while distance >= nearest:
        partial = partial + exchanged(partial, kinds, distance)
        distance //= 2
    return partial


def stepped(block, kinds=(), distance=0):
    return routed(block, lambda k, p: (k + 1, p ^ distance if k % 2 in kinds else p))


def assemble_kernel(counts, kind_ref, *refs):
    ins, (out_ref, made, sems) = list(refs[:-3]), refs[-3:]
    parts = [[ins.pop(0) for _ in range(count)] for count in counts]
    odd = kind_ref[0] == 1
    copies = []
    for side in (1, 0):
        early, near, far = parts[3 * side : 3 * side + 3]
        for c in (0, 1):
            terms = near[0][c], far[0][c] + far[1][c]
            late = jnp.where(odd, terms[1 - side], terms[side])
            matrix = jnp.concatenate([ref[c] for ref in early] + [late], axis=0)
            if side == 0:
                matrix = matrix.T
            elif c == 1:
                matrix = -matrix
            made[2 * side + c] = matrix
            copies.append(
                pltpu.make_async_copy(
                    made.at[2 * side + c], out_ref.at[0, side, c], sems.at[2 * side + c]
                )
            )
            copies[-1].start()
    for copy in copies:
        copy.wait()


def assembled(*parts):
    bands = parts[0][0].shape[2]
    counts = [len(part) for part in parts]
    kind = (lax.axis_index("ka") % 2).astype(jnp.int32).reshape(1)
    return pl.pallas_call(
        functools.partial(assemble_kernel, counts),
        out_shape=jax.ShapeDtypeStruct((1, 2, 2, bands, bands), jnp.float32),
        in_specs=[pl.BlockSpec(memory_space=pltpu.SMEM)] + [WHOLE] * sum(counts),
        out_specs=ANYWHERE,
        scratch_shapes=[
            pltpu.VMEM((4, bands, bands), jnp.float32),
            pltpu.SemaphoreType.DMA((4,)),
        ],
        compiler_params=pltpu.CompilerParams(vmem_limit_bytes=16 * MIB),
        cost_estimate=pl.CostEstimate(flops=0, bytes_accessed=1024, transcendentals=0),
        name="assemble",
    )(kind, *[array for part in parts for array in part])


def local(coefficients, shifts):
    bands, width = coefficients.shape[2:]
    unit = bands // sum(SIXTEENTHS)
    edges = [0]
    for size in SIXTEENTHS:
        edges.append(edges[-1] + size * unit)
    late = width // PWB * 3 // 4 * PWB
    coefficients = pltpu.with_memory_space_constraint(coefficients, pltpu.HBM)
    placed = pltpu.with_memory_space_constraint(placed_bands(coefficients, shifts), pltpu.VMEM)
    blocks, arrived, whole = [], [], []

    def send(chunk, low, high, *others):
        some = slice(edges[chunk], edges[chunk + 1])
        blocks.append(cut(coefficients, some, slice(low, high), *blocks[-1:], *others))
        return blocks[-1]

    for chunk in range(3):
        arrived.append(fetched(send(chunk, 0, width)))
    arrived.append(fetched(send(3, 0, width, arrived[0], placed)))
    near_block = swapped(send(4, 0, width))
    whole.append(summed_over_pw(correlate(placed, arrived[0]), ALL))
    near = summed_over_pw(correlate(placed, near_block, whole[0]), EVEN)
    near_before = swapped(near)
    arrived.append(fetched(send(4, 0, late, arrived[1], near)))
    whole.append(summed_over_pw(correlate(placed, arrived[1], near), ALL))
    arrived.append(fetched(send(4, late, width, arrived[2], whole[1])))
    for chunk in (2, 3):
        partial = correlate(placed, arrived[chunk], whole[-1], near_before)
        whole.append(summed_over_pw(partial, ALL))
    halves = [jnp.concatenate(whole[:2], axis=1), jnp.concatenate(whole[2:], axis=1)]
    last = correlate(placed, arrived[4], *halves)
    last, *halves = correlate(placed, arrived[5], first=late, begun=last, held=halves)
    halves_before = [stepped(half) for half in halves]
    last = summed_over_pw(last, ODD, nearest=2)
    ahead = [last, exchanged(last, ODD, 1)]
    behind = [stepped(last), stepped(last, ODD, 1)]
    return assembled(halves, [near], ahead, halves_before, [near_before], behind)


def solution(mesh):
    return jax.shard_map(
        local,
        mesh=mesh,
        in_specs=(P(("groups", "ka"), None, None, "pw"), P(("groups", "ka"), None, "pw")),
        out_specs=P(("groups", "ka"), None, None, None, None),
        check_vma=False,
    )
```

```python
import functools

import jax
import jax.numpy as jnp
from jax import lax
from jax.experimental import pallas as pl
from jax.experimental.pallas import tpu as pltpu
from jax.sharding import PartitionSpec as P

PWB = 256
SIXTEENTHS = (6, 4, 2, 2, 2)
PIECES = 1
MIB = 1 << 20
ANYWHERE = pl.BlockSpec(memory_space=pl.ANY)
WHOLE = pl.BlockSpec(memory_space=pltpu.VMEM)


def moved(block, axis, distance):
    count = lax.axis_size(axis)
    return lax.ppermute(block, axis, [(i, (i + distance) % count) for i in range(count)])


def cut_kernel(bands, waves, *refs):
    own_ref, out_ref, sems = refs[0], refs[-2], refs[-1]
    copies = [
        pltpu.make_async_copy(own_ref.at[0, c, bands, waves], out_ref.at[c], sems.at[c])
        for c in range(2)
    ]
    for copy in copies:
        copy.start()
    for copy in copies:
        copy.wait()


def cut(coefficients, bands, waves, *others):
    shape = (2, bands.stop - bands.start, waves.stop - waves.start)
    return pl.pallas_call(
        functools.partial(cut_kernel, bands, waves),
        out_shape=jax.ShapeDtypeStruct(shape, coefficients.dtype),
        in_specs=[ANYWHERE] * (1 + len(others)),
        out_specs=ANYWHERE,
        scratch_shapes=[pltpu.SemaphoreType.DMA((2,))],
        compiler_params=pltpu.CompilerParams(vmem_limit_bytes=MIB),
        cost_estimate=pl.CostEstimate(flops=0, bytes_accessed=1024, transcendentals=0),
        name="cut",
    )(coefficients, *others)


def place_kernel(own_ref, shift_ref, out_ref):
    bands, width = own_ref.shape[2:]
    base = pl.program_id(0) * width
    goal = lax.broadcasted_iota(jnp.int32, (PWB, PWB), 0)
    for block in range(width // PWB):
        here = pl.ds(block * PWB, PWB)
        inside = shift_ref[0, 0:1, here] & (PWB - 1)
        selector = (goal == inside).astype(jnp.float32).astype(jnp.bfloat16)
        rows = own_ref[0, :, :, here].reshape(2 * bands, PWB)
        placed = lax.dot_general(
            selector, rows, (((1,), (1,)), ((), ())), preferred_element_type=jnp.float32
        )
        there = pl.multiple_of(base + block * PWB, PWB)
        out_ref[pl.ds(there, PWB), :] = placed.astype(jnp.bfloat16)


def placed_bands(coefficients, shifts):
    bands, width = coefficients.shape[2:]
    step = 4 * PWB if width % (4 * PWB) == 0 else PWB
    return pl.pallas_call(
        place_kernel,
        grid=(width // step,),
        out_shape=pltpu.VMEM((width, 2 * bands), jnp.bfloat16),
        in_specs=[
            pl.BlockSpec((1, 2, bands, step), lambda g: (0, 0, 0, g)),
            pl.BlockSpec((1, 2, step), lambda g: (0, 0, g)),
        ],
        out_specs=WHOLE,
        compiler_params=pltpu.CompilerParams(vmem_limit_bytes=16 * MIB),
        cost_estimate=pl.CostEstimate(flops=0, bytes_accessed=1024, transcendentals=0),
        name="place",
    )(coefficients, shifts)


def correlate_kernel(first, depth, begun, held, placed_ref, block_ref, *refs):
    out_ref, total = refs[-2 - held], refs[-1]
    some, width = block_ref.shape[1:]
    bands = out_ref.shape[2]

    def product_of(start):
        return jnp.dot(
            block_ref[:, :, pl.ds(start, depth)].reshape(2 * some, depth),
            placed_ref[pl.ds(first + start, depth), :],
            preferred_element_type=jnp.float32,
        )

    total[...] = product_of(0)

    @pl.loop(1, width // depth)
    def _(step):
        total[...] += product_of(pl.multiple_of(step * depth, depth))

    real_part = total[:some, :bands] + total[some:, bands:]
    imag_part = total[some:, :bands] - total[:some, bands:]
    out_ref[0] = refs[0][0] + real_part if begun else real_part
    out_ref[1] = refs[0][1] + imag_part if begun else imag_part


def correlate(placed, block, *others, first=0, begun=None, held=()):
    some, width = block.shape[1:]
    bands = placed.shape[1] // 2
    depth = width
    while depth % (2 * PWB) == 0 and some * depth > 1 << 19:
        depth //= 2
    block = pltpu.with_memory_space_constraint(block, pltpu.VMEM)
    ins = [placed, block] if begun is None else [placed, block, begun]
    in_specs = [WHOLE] * len(ins) + [ANYWHERE] * (len(others) + len(held))
    before = len(ins) + len(others)
    product = jax.ShapeDtypeStruct((2, some, bands), jnp.float32)
    out = pl.pallas_call(
        functools.partial(correlate_kernel, first, depth, begun is not None, len(held)),
        out_shape=[product] + [jax.ShapeDtypeStruct(kept.shape, kept.dtype) for kept in held],
        in_specs=in_specs,
        out_specs=[WHOLE] + [ANYWHERE] * len(held),
        scratch_shapes=[pltpu.VMEM((2 * some, 2 * bands), jnp.float32)],
        input_output_aliases={before + index: 1 + index for index in range(len(held))},
        compiler_params=pltpu.CompilerParams(vmem_limit_bytes=16 * MIB),
        cost_estimate=pl.CostEstimate(flops=0, bytes_accessed=1024, transcendentals=0),
        name="correlate",
    )(*ins, *others, *held)
    return out if held else out[0]


def summed_over_pw(partial):
    pw = lax.axis_size("pw")
    if pw & (pw - 1):
        return partial + sum(moved(partial, "pw", d) for d in range(1, pw))
    distance = pw // 2
    while distance:
        partial = partial + lax.ppermute(partial, "pw", [(i, i ^ distance) for i in range(pw)])
        distance //= 2
    return partial


def sums_here_and_next(partial):
    ka, pw = lax.axis_size("ka"), lax.axis_size("pw")
    if pw & (pw - 1) or pw == 1:
        whole = summed_over_pw(partial)
        return [whole], [moved(whole, "ka", 1)]
    distance = pw // 2
    while distance > 1:
        partial = partial + lax.ppermute(partial, "pw", [(i, i ^ distance) for i in range(pw)])
        distance //= 2
    here = lax.ppermute(partial, "pw", [(i, i ^ 1) for i in range(pw)])
    across = [(k * pw + p, (k + 1) % ka * pw + (p ^ 1)) for k in range(ka) for p in range(pw)]
    before = [moved(partial, "ka", 1), lax.ppermute(partial, ("ka", "pw"), across)]
    return [partial, here], before


def assemble_kernel(counts, *refs):
    ins, (out_ref, made, sems) = list(refs[:-3]), refs[-3:]
    most, most_before, *last_refs = [[ins.pop(0) for _ in range(count)] for count in counts]
    copies = []
    for side in (1, 0):
        for c in (0, 1):
            early = [ref[c] for ref in (most, most_before)[side]]
            late = sum(ref[c] for ref in last_refs[side])
            matrix = jnp.concatenate([*early, late], axis=0)
            if side == 0:
                matrix = matrix.T
            elif c == 1:
                matrix = -matrix
            made[2 * side + c] = matrix
            copies.append(
                pltpu.make_async_copy(
                    made.at[2 * side + c], out_ref.at[0, side, c], sems.at[2 * side + c]
                )
            )
            copies[-1].start()
    for copy in copies:
        copy.wait()


def assembled(*parts):
    bands = parts[0][0].shape[2]
    counts = [len(part) for part in parts]
    return pl.pallas_call(
        functools.partial(assemble_kernel, counts),
        out_shape=jax.ShapeDtypeStruct((1, 2, 2, bands, bands), jnp.float32),
        in_specs=[WHOLE] * sum(counts),
        out_specs=ANYWHERE,
        scratch_shapes=[
            pltpu.VMEM((4, bands, bands), jnp.float32),
            pltpu.SemaphoreType.DMA((4,)),
        ],
        compiler_params=pltpu.CompilerParams(vmem_limit_bytes=16 * MIB),
        cost_estimate=pl.CostEstimate(flops=0, bytes_accessed=1024, transcendentals=0),
        name="assemble",
    )(*[array for part in parts for array in part])


def local(coefficients, shifts):
    bands, width = coefficients.shape[2:]
    unit = bands // sum(SIXTEENTHS)
    edges = [0]
    for size in SIXTEENTHS:
        edges.append(edges[-1] + size * unit)
    late = width // PWB * 3 // 4 * PWB
    coefficients = pltpu.with_memory_space_constraint(coefficients, pltpu.HBM)
    placed = pltpu.with_memory_space_constraint(placed_bands(coefficients, shifts), pltpu.VMEM)
    blocks, arrived, whole = [], [], []

    def send(chunk, low, high, *others):
        some = slice(edges[chunk], edges[chunk + 1])
        blocks.append(cut(coefficients, some, slice(low, high), *blocks[-1:], *others))
        arrived.append(moved(blocks[-1], "ka", -1))

    for chunk in range(3):
        send(chunk, 0, width)
    send(3, 0, width, arrived[0], placed)
    for chunk in range(4):
        if chunk == 1:
            send(4, 0, late, arrived[1], whole[0])
        if chunk == 2:
            send(4, late, width, arrived[2], whole[1])
        whole.append(summed_over_pw(correlate(placed, arrived[chunk], *whole[-1:])))
    pieces = jnp.split(jnp.concatenate(whole, axis=1), PIECES, axis=1)
    last = correlate(placed, arrived[4], *pieces)
    last, *pieces = correlate(placed, arrived[5], first=late, begun=last, held=pieces)
    pieces_before = [moved(piece, "ka", 1) for piece in pieces]
    return assembled(pieces, pieces_before, *sums_here_and_next(last))


def solution(mesh):
    return jax.shard_map(
        local,
        mesh=mesh,
        in_specs=(P(("groups", "ka"), None, None, "pw"), P(("groups", "ka"), None, "pw")),
        out_specs=P(("groups", "ka"), None, None, None, None),
        check_vma=False,
    )
```

```python
import functools

import jax
import jax.numpy as jnp
from jax import lax
from jax.experimental import pallas as pl
from jax.experimental.pallas import tpu as pltpu
from jax.sharding import PartitionSpec as P

PWB = 256
SIXTEENTHS = (6, 4, 3, 2, 1)
MIB = 1 << 20
ANYWHERE = pl.BlockSpec(memory_space=pl.ANY)
WHOLE = pl.BlockSpec(memory_space=pltpu.VMEM)


def moved(block, axis, distance):
    count = lax.axis_size(axis)
    return lax.ppermute(block, axis, [(i, (i + distance) % count) for i in range(count)])


def cut_kernel(bands, waves, *refs):
    own_ref, out_ref, sems = refs[0], refs[-2], refs[-1]
    copies = [
        pltpu.make_async_copy(own_ref.at[0, c, bands, waves], out_ref.at[c], sems.at[c])
        for c in range(2)
    ]
    for copy in copies:
        copy.start()
    for copy in copies:
        copy.wait()


def cut(coefficients, bands, waves, *others):
    shape = (2, bands.stop - bands.start, waves.stop - waves.start)
    return pl.pallas_call(
        functools.partial(cut_kernel, bands, waves),
        out_shape=jax.ShapeDtypeStruct(shape, coefficients.dtype),
        in_specs=[ANYWHERE] * (1 + len(others)),
        out_specs=ANYWHERE,
        scratch_shapes=[pltpu.SemaphoreType.DMA((2,))],
        compiler_params=pltpu.CompilerParams(vmem_limit_bytes=MIB),
        cost_estimate=pl.CostEstimate(flops=0, bytes_accessed=1024, transcendentals=0),
        name="cut",
    )(coefficients, *others)


def place_kernel(own_ref, shift_ref, out_ref):
    bands, width = own_ref.shape[2:]
    base = pl.program_id(0) * width
    goal = lax.broadcasted_iota(jnp.int32, (PWB, PWB), 0)
    for block in range(width // PWB):
        here = pl.ds(block * PWB, PWB)
        inside = shift_ref[0, 0:1, here] & (PWB - 1)
        selector = (goal == inside).astype(jnp.float32).astype(jnp.bfloat16)
        rows = own_ref[0, :, :, here].reshape(2 * bands, PWB)
        placed = lax.dot_general(
            selector, rows, (((1,), (1,)), ((), ())), preferred_element_type=jnp.float32
        )
        there = pl.multiple_of(base + block * PWB, PWB)
        out_ref[pl.ds(there, PWB), :] = placed.astype(jnp.bfloat16)


def placed_bands(coefficients, shifts):
    bands, width = coefficients.shape[2:]
    step = 4 * PWB if width % (4 * PWB) == 0 else PWB
    return pl.pallas_call(
        place_kernel,
        grid=(width // step,),
        out_shape=pltpu.VMEM((width, 2 * bands), jnp.bfloat16),
        in_specs=[
            pl.BlockSpec((1, 2, bands, step), lambda g: (0, 0, 0, g)),
            pl.BlockSpec((1, 2, step), lambda g: (0, 0, g)),
        ],
        out_specs=WHOLE,
        compiler_params=pltpu.CompilerParams(vmem_limit_bytes=16 * MIB),
        cost_estimate=pl.CostEstimate(flops=0, bytes_accessed=1024, transcendentals=0),
        name="place",
    )(coefficients, shifts)


def correlate_kernel(first, depth, begun, held, placed_ref, block_ref, *refs):
    out_ref, total = refs[-2 - held], refs[-1]
    some, width = block_ref.shape[1:]
    bands = out_ref.shape[2]

    def product_of(start):
        return jnp.dot(
            block_ref[:, :, pl.ds(start, depth)].reshape(2 * some, depth),
            placed_ref[pl.ds(first + start, depth), :],
            preferred_element_type=jnp.float32,
        )

    total[...] = product_of(0)

    @pl.loop(1, width // depth)
    def _(step):
        total[...] += product_of(pl.multiple_of(step * depth, depth))

    real_part = total[:some, :bands] + total[some:, bands:]
    imag_part = total[some:, :bands] - total[:some, bands:]
    out_ref[0] = refs[0][0] + real_part if begun else real_part
    out_ref[1] = refs[0][1] + imag_part if begun else imag_part


def correlate(placed, block, *others, first=0, begun=None, held=()):
    some, width = block.shape[1:]
    bands = placed.shape[1] // 2
    depth = width
    while depth % (2 * PWB) == 0 and some * depth > 1 << 19:
        depth //= 2
    block = pltpu.with_memory_space_constraint(block, pltpu.VMEM)
    ins = [placed, block] if begun is None else [placed, block, begun]
    in_specs = [WHOLE] * len(ins) + [ANYWHERE] * (len(others) + len(held))
    before = len(ins) + len(others)
    product = jax.ShapeDtypeStruct((2, some, bands), jnp.float32)
    out = pl.pallas_call(
        functools.partial(correlate_kernel, first, depth, begun is not None, len(held)),
        out_shape=[product] + [jax.ShapeDtypeStruct(kept.shape, kept.dtype) for kept in held],
        in_specs=in_specs,
        out_specs=[WHOLE] + [ANYWHERE] * len(held),
        scratch_shapes=[pltpu.VMEM((2 * some, 2 * bands), jnp.float32)],
        input_output_aliases={before + index: 1 + index for index in range(len(held))},
        compiler_params=pltpu.CompilerParams(vmem_limit_bytes=16 * MIB),
        cost_estimate=pl.CostEstimate(flops=0, bytes_accessed=1024, transcendentals=0),
        name="correlate",
    )(*ins, *others, *held)
    return out if held else out[0]


def exchanged(block, distance):
    return lax.ppermute(block, "pw", [(i, i ^ distance) for i in range(lax.axis_size("pw"))])


def summed_over_pw(partial, nearest=1, farthest=None):
    distance = farthest or lax.axis_size("pw") // 2
    while distance >= nearest:
        partial = partial + exchanged(partial, distance)
        distance //= 2
    return partial


def crossed(block):
    ka, pw = lax.axis_size("ka"), lax.axis_size("pw")
    route = [(k * pw + p, (k + 1) % ka * pw + (p ^ 1)) for k in range(ka) for p in range(pw)]
    return lax.ppermute(block, ("ka", "pw"), route)


def assemble_kernel(
    most_ref, some_ref, last_ref, here_ref, most_before_ref, joint_ref, crossed_ref, out_ref, made, sems
):
    some = some_ref.shape[1]
    copies = []
    for side in (1, 0):
        for c in (0, 1):
            if side == 1:
                late = joint_ref[c, some:] + crossed_ref[c]
                matrix = jnp.concatenate([most_before_ref[c], joint_ref[c, :some], late], axis=0)
                matrix = -matrix if c == 1 else matrix
            else:
                late = last_ref[c] + here_ref[c]
                matrix = jnp.concatenate([most_ref[c], some_ref[c], late], axis=0).T
            made[2 * side + c] = matrix
            copies.append(
                pltpu.make_async_copy(
                    made.at[2 * side + c], out_ref.at[0, side, c], sems.at[2 * side + c]
                )
            )
            copies[-1].start()
    for copy in copies:
        copy.wait()


def assembled(*parts):
    bands = parts[0].shape[2]
    return pl.pallas_call(
        assemble_kernel,
        out_shape=jax.ShapeDtypeStruct((1, 2, 2, bands, bands), jnp.float32),
        in_specs=[WHOLE] * len(parts),
        out_specs=ANYWHERE,
        scratch_shapes=[
            pltpu.VMEM((4, bands, bands), jnp.float32),
            pltpu.SemaphoreType.DMA((4,)),
        ],
        compiler_params=pltpu.CompilerParams(vmem_limit_bytes=16 * MIB),
        cost_estimate=pl.CostEstimate(flops=0, bytes_accessed=1024, transcendentals=0),
        name="assemble",
    )(*parts)


def local(coefficients, shifts):
    bands, width = coefficients.shape[2:]
    unit = bands // sum(SIXTEENTHS)
    edges = [0]
    for size in SIXTEENTHS:
        edges.append(edges[-1] + size * unit)
    half, late = (width // PWB * quarters // 4 * PWB for quarters in (2, 3))
    coefficients = pltpu.with_memory_space_constraint(coefficients, pltpu.HBM)
    placed = pltpu.with_memory_space_constraint(placed_bands(coefficients, shifts), pltpu.VMEM)
    blocks, arrived, whole = [], [], []

    def send(chunk, low, high, *others):
        some = slice(edges[chunk], edges[chunk + 1])
        blocks.append(cut(coefficients, some, slice(low, high), *blocks[-1:], *others))
        arrived.append(moved(blocks[-1], "ka", -1))

    for chunk in range(3):
        send(chunk, 0, width)
    send(3, 0, half, arrived[0], placed)
    whole.append(summed_over_pw(correlate(placed, arrived[0])))
    send(3, half, width, arrived[1], whole[0])
    whole.append(summed_over_pw(correlate(placed, arrived[1], whole[0])))
    send(4, 0, late, arrived[2], whole[1])
    whole.append(summed_over_pw(correlate(placed, arrived[2], whole[1])))
    send(4, late, width, arrived[2], whole[1])
    some = correlate(placed, arrived[3], whole[2])
    some = correlate(placed, arrived[4], first=half, begun=some)
    farthest = lax.axis_size("pw") // 2
    more = exchanged(some, farthest)
    most = jnp.concatenate(whole, axis=1)
    last, some = correlate(placed, arrived[5], most, held=[some])
    some = summed_over_pw(some + more, nearest=2, farthest=farthest // 2)
    last, some, most = correlate(placed, arrived[6], first=late, begun=last, held=[some, most])
    most_before = moved(most, "ka", 1)
    last = summed_over_pw(last, nearest=2)
    some = some + exchanged(some, 1)
    joint = moved(jnp.concatenate([some, last], axis=1), "ka", 1)
    return assembled(most, some, last, exchanged(last, 1), most_before, joint, crossed(last))


def solution(mesh):
    return jax.shard_map(
        local,
        mesh=mesh,
        in_specs=(P(("groups", "ka"), None, None, "pw"), P(("groups", "ka"), None, "pw")),
        out_specs=P(("groups", "ka"), None, None, None, None),
        check_vma=False,
    )
```

```python
import functools

import jax
import jax.numpy as jnp
from jax import lax
from jax.experimental import pallas as pl
from jax.experimental.pallas import tpu as pltpu
from jax.sharding import PartitionSpec as P

PWB = 256
SIXTEENTHS = (6, 4, 2, 2, 2)
MIB = 1 << 20
ANYWHERE = pl.BlockSpec(memory_space=pl.ANY)
WHOLE = pl.BlockSpec(memory_space=pltpu.VMEM)


def moved(block, axis, distance):
    count = lax.axis_size(axis)
    return lax.ppermute(block, axis, [(i, (i + distance) % count) for i in range(count)])


def cut_kernel(bands, waves, *refs):
    own_ref, out_ref, sems = refs[0], refs[-2], refs[-1]
    copies = [
        pltpu.make_async_copy(own_ref.at[0, c, bands, waves], out_ref.at[c], sems.at[c])
        for c in range(2)
    ]
    for copy in copies:
        copy.start()
    for copy in copies:
        copy.wait()


def cut(coefficients, bands, waves, *others):
    shape = (2, bands.stop - bands.start, waves.stop - waves.start)
    return pl.pallas_call(
        functools.partial(cut_kernel, bands, waves),
        out_shape=jax.ShapeDtypeStruct(shape, coefficients.dtype),
        in_specs=[ANYWHERE] * (1 + len(others)),
        out_specs=ANYWHERE,
        scratch_shapes=[pltpu.SemaphoreType.DMA((2,))],
        compiler_params=pltpu.CompilerParams(vmem_limit_bytes=MIB),
        cost_estimate=pl.CostEstimate(flops=0, bytes_accessed=1024, transcendentals=0),
        name="cut",
    )(coefficients, *others)


def place_kernel(own_ref, shift_ref, *refs):
    out_ref = refs[-1]
    bands, width = own_ref.shape[2:]
    base = pl.program_id(0) * width
    goal = lax.broadcasted_iota(jnp.int32, (PWB, PWB), 0)
    for block in range(width // PWB):
        here = pl.ds(block * PWB, PWB)
        inside = shift_ref[0, 0:1, here] & (PWB - 1)
        selector = (goal == inside).astype(jnp.float32).astype(jnp.bfloat16)
        rows = own_ref[0, :, :, here].reshape(2 * bands, PWB)
        placed = lax.dot_general(
            selector, rows, (((1,), (1,)), ((), ())), preferred_element_type=jnp.float32
        )
        there = pl.multiple_of(base + block * PWB, PWB)
        out_ref[pl.ds(there, PWB), :] = placed.astype(jnp.bfloat16)


def placed_bands(coefficients, shifts, *others):
    bands, width = coefficients.shape[2:]
    step = 4 * PWB if width % (4 * PWB) == 0 else PWB
    return pl.pallas_call(
        place_kernel,
        grid=(width // step,),
        out_shape=pltpu.VMEM((width, 2 * bands), jnp.bfloat16),
        in_specs=[
            pl.BlockSpec((1, 2, bands, step), lambda g: (0, 0, 0, g)),
            pl.BlockSpec((1, 2, step), lambda g: (0, 0, g)),
        ]
        + [ANYWHERE] * len(others),
        out_specs=WHOLE,
        compiler_params=pltpu.CompilerParams(vmem_limit_bytes=16 * MIB),
        cost_estimate=pl.CostEstimate(flops=0, bytes_accessed=1024, transcendentals=0),
        name="place",
    )(coefficients, shifts, *others)


def correlate_kernel(first, depth, begun, held, placed_ref, block_ref, *refs):
    out_ref, total = refs[-2 - held], refs[-1]
    some, width = block_ref.shape[1:]
    bands = out_ref.shape[2]

    def product_of(start):
        return jnp.dot(
            block_ref[:, :, pl.ds(start, depth)].reshape(2 * some, depth),
            placed_ref[pl.ds(first + start, depth), :],
            preferred_element_type=jnp.float32,
        )

    total[...] = product_of(0)

    @pl.loop(1, width // depth)
    def _(step):
        total[...] += product_of(pl.multiple_of(step * depth, depth))

    real_part = total[:some, :bands] + total[some:, bands:]
    imag_part = total[some:, :bands] - total[:some, bands:]
    out_ref[0] = refs[0][0] + real_part if begun else real_part
    out_ref[1] = refs[0][1] + imag_part if begun else imag_part


def correlate(placed, block, *others, first=0, begun=None, held=()):
    some, width = block.shape[1:]
    bands = placed.shape[1] // 2
    depth = width
    while depth % (2 * PWB) == 0 and some * depth > 1 << 19:
        depth //= 2
    block = pltpu.with_memory_space_constraint(block, pltpu.VMEM)
    ins = [placed, block] if begun is None else [placed, block, begun]
    in_specs = [WHOLE] * len(ins) + [ANYWHERE] * (len(others) + len(held))
    before = len(ins) + len(others)
    product = jax.ShapeDtypeStruct((2, some, bands), jnp.float32)
    out = pl.pallas_call(
        functools.partial(correlate_kernel, first, depth, begun is not None, len(held)),
        out_shape=[product] + [jax.ShapeDtypeStruct(kept.shape, kept.dtype) for kept in held],
        in_specs=in_specs,
        out_specs=[WHOLE] + [ANYWHERE] * len(held),
        scratch_shapes=[pltpu.VMEM((2 * some, 2 * bands), jnp.float32)],
        input_output_aliases={before + index: 1 + index for index in range(len(held))},
        compiler_params=pltpu.CompilerParams(vmem_limit_bytes=16 * MIB),
        cost_estimate=pl.CostEstimate(flops=0, bytes_accessed=1024, transcendentals=0),
        name="correlate",
    )(*ins, *others, *held)
    return out if held else out[0]


def summed_over_pw(partial):
    pw = lax.axis_size("pw")
    if pw & (pw - 1):
        return partial + sum(moved(partial, "pw", d) for d in range(1, pw))
    distance = pw // 2
    while distance:
        partial = partial + lax.ppermute(partial, "pw", [(i, i ^ distance) for i in range(pw)])
        distance //= 2
    return partial


def sums_here_and_next(partial):
    ka, pw = lax.axis_size("ka"), lax.axis_size("pw")
    if pw & (pw - 1) or pw == 1:
        whole = summed_over_pw(partial)
        return [whole], [moved(whole, "ka", 1)]
    distance = pw // 2
    while distance > 1:
        partial = partial + lax.ppermute(partial, "pw", [(i, i ^ distance) for i in range(pw)])
        distance //= 2
    here = lax.ppermute(partial, "pw", [(i, i ^ 1) for i in range(pw)])
    across = [(k * pw + p, (k + 1) % ka * pw + (p ^ 1)) for k in range(ka) for p in range(pw)]
    before = [moved(partial, "ka", 1), lax.ppermute(partial, ("ka", "pw"), across)]
    return [partial, here], before


def assemble_kernel(counts, *refs):
    ins, (out_ref, made, sems) = list(refs[:-3]), refs[-3:]
    most, most_before, *last_refs = [[ins.pop(0) for _ in range(count)] for count in counts]
    copies = []
    for side in (1, 0):
        for c in (0, 1):
            early = [ref[c] for ref in (most, most_before)[side]]
            late = sum(ref[c] for ref in last_refs[side])
            matrix = jnp.concatenate([*early, late], axis=0)
            if side == 0:
                matrix = matrix.T
            elif c == 1:
                matrix = -matrix
            made[2 * side + c] = matrix
            copies.append(
                pltpu.make_async_copy(
                    made.at[2 * side + c], out_ref.at[0, side, c], sems.at[2 * side + c]
                )
            )
            copies[-1].start()
    for copy in copies:
        copy.wait()


def assembled(*parts):
    bands = parts[0][0].shape[2]
    counts = [len(part) for part in parts]
    return pl.pallas_call(
        functools.partial(assemble_kernel, counts),
        out_shape=jax.ShapeDtypeStruct((1, 2, 2, bands, bands), jnp.float32),
        in_specs=[WHOLE] * sum(counts),
        out_specs=ANYWHERE,
        scratch_shapes=[
            pltpu.VMEM((4, bands, bands), jnp.float32),
            pltpu.SemaphoreType.DMA((4,)),
        ],
        compiler_params=pltpu.CompilerParams(vmem_limit_bytes=16 * MIB),
        cost_estimate=pl.CostEstimate(flops=0, bytes_accessed=1024, transcendentals=0),
        name="assemble",
    )(*[array for part in parts for array in part])


def local(coefficients, shifts):
    bands, width = coefficients.shape[2:]
    unit = bands // sum(SIXTEENTHS)
    edges = [0]
    for size in SIXTEENTHS:
        edges.append(edges[-1] + size * unit)
    late = width // PWB * 3 // 4 * PWB
    coefficients = pltpu.with_memory_space_constraint(coefficients, pltpu.HBM)
    ranges = [(chunk, 0, width) for chunk in range(4)] + [(4, 0, late), (4, late, width)]
    blocks = []
    for chunk, low, high in ranges:
        some = slice(edges[chunk], edges[chunk + 1])
        blocks.append(cut(coefficients, some, slice(low, high), *blocks[-1:]))
    placed = placed_bands(coefficients, shifts, *blocks[-1:])
    placed = pltpu.with_memory_space_constraint(placed, pltpu.VMEM)
    arrived = [moved(block, "ka", -1) for block in blocks[:3]]
    whole = []
    for chunk in range(4):
        waiting = blocks[3 + chunk : 4 + chunk]
        partial = correlate(placed, arrived[chunk], *whole[-1:], held=waiting)
        if waiting:
            partial, waiting = partial
            arrived.append(moved(waiting, "ka", -1))
        whole.append(summed_over_pw(partial))
    most = jnp.concatenate(whole, axis=1)
    last = correlate(placed, arrived[4], most)
    last, most = correlate(placed, arrived[5], first=late, begun=last, held=[most])
    return assembled([most], [moved(most, "ka", 1)], *sums_here_and_next(last))


def solution(mesh):
    return jax.shard_map(
        local,
        mesh=mesh,
        in_specs=(P(("groups", "ka"), None, None, "pw"), P(("groups", "ka"), None, "pw")),
        out_specs=P(("groups", "ka"), None, None, None, None),
        check_vma=False,
    )
```

```python
import functools

import jax
import jax.numpy as jnp
from jax import lax
from jax.experimental import pallas as pl
from jax.experimental.pallas import tpu as pltpu
from jax.sharding import PartitionSpec as P

PWB = 256
SIXTEENTHS = (6, 4, 2, 2, 2)
MIB = 1 << 20
ANYWHERE = pl.BlockSpec(memory_space=pl.ANY)
WHOLE = pl.BlockSpec(memory_space=pltpu.VMEM)


def moved(block, axis, distance):
    count = lax.axis_size(axis)
    return lax.ppermute(block, axis, [(i, (i + distance) % count) for i in range(count)])


def cut_kernel(bands, waves, *refs):
    own_ref, out_ref, sems = refs[0], refs[-2], refs[-1]
    copies = [
        pltpu.make_async_copy(own_ref.at[0, c, bands, waves], out_ref.at[c], sems.at[c])
        for c in range(2)
    ]
    for copy in copies:
        copy.start()
    for copy in copies:
        copy.wait()


def cut(coefficients, bands, waves, *others):
    shape = (2, bands.stop - bands.start, waves.stop - waves.start)
    return pl.pallas_call(
        functools.partial(cut_kernel, bands, waves),
        out_shape=jax.ShapeDtypeStruct(shape, coefficients.dtype),
        in_specs=[ANYWHERE] * (1 + len(others)),
        out_specs=ANYWHERE,
        scratch_shapes=[pltpu.SemaphoreType.DMA((2,))],
        compiler_params=pltpu.CompilerParams(vmem_limit_bytes=MIB),
        cost_estimate=pl.CostEstimate(flops=0, bytes_accessed=1024, transcendentals=0),
        name="cut",
    )(coefficients, *others)


def place_kernel(own_ref, shift_ref, *refs):
    out_ref = refs[-1]
    bands, width = own_ref.shape[2:]
    base = pl.program_id(0) * width
    goal = lax.broadcasted_iota(jnp.int32, (PWB, PWB), 0)
    for block in range(width // PWB):
        here = pl.ds(block * PWB, PWB)
        inside = shift_ref[0, 0:1, here] & (PWB - 1)
        selector = (goal == inside).astype(jnp.float32).astype(jnp.bfloat16)
        rows = own_ref[0, :, :, here].reshape(2 * bands, PWB)
        placed = lax.dot_general(
            selector, rows, (((1,), (1,)), ((), ())), preferred_element_type=jnp.float32
        )
        there = pl.multiple_of(base + block * PWB, PWB)
        out_ref[pl.ds(there, PWB), :] = placed.astype(jnp.bfloat16)


def placed_bands(coefficients, shifts, *others):
    bands, width = coefficients.shape[2:]
    step = 4 * PWB if width % (4 * PWB) == 0 else PWB
    return pl.pallas_call(
        place_kernel,
        grid=(width // step,),
        out_shape=pltpu.VMEM((width, 2 * bands), jnp.bfloat16),
        in_specs=[
            pl.BlockSpec((1, 2, bands, step), lambda g: (0, 0, 0, g)),
            pl.BlockSpec((1, 2, step), lambda g: (0, 0, g)),
        ]
        + [ANYWHERE] * len(others),
        out_specs=WHOLE,
        compiler_params=pltpu.CompilerParams(vmem_limit_bytes=16 * MIB),
        cost_estimate=pl.CostEstimate(flops=0, bytes_accessed=1024, transcendentals=0),
        name="place",
    )(coefficients, shifts, *others)


def correlate_kernel(first, depth, begun, held, placed_ref, block_ref, *refs):
    out_ref, total = refs[-2 - held], refs[-1]
    some, width = block_ref.shape[1:]
    bands = out_ref.shape[2]

    def product_of(start):
        return jnp.dot(
            block_ref[:, :, pl.ds(start, depth)].reshape(2 * some, depth),
            placed_ref[pl.ds(first + start, depth), :],
            preferred_element_type=jnp.float32,
        )

    total[...] = product_of(0)

    @pl.loop(1, width // depth)
    def _(step):
        total[...] += product_of(pl.multiple_of(step * depth, depth))

    real_part = total[:some, :bands] + total[some:, bands:]
    imag_part = total[some:, :bands] - total[:some, bands:]
    out_ref[0] = refs[0][0] + real_part if begun else real_part
    out_ref[1] = refs[0][1] + imag_part if begun else imag_part


def correlate(placed, block, *others, first=0, begun=None, held=()):
    some, width = block.shape[1:]
    bands = placed.shape[1] // 2
    depth = width
    while depth % (2 * PWB) == 0 and some * depth > 1 << 19:
        depth //= 2
    block = pltpu.with_memory_space_constraint(block, pltpu.VMEM)
    ins = [placed, block] if begun is None else [placed, block, begun]
    in_specs = [WHOLE] * len(ins) + [ANYWHERE] * (len(others) + len(held))
    before = len(ins) + len(others)
    product = jax.ShapeDtypeStruct((2, some, bands), jnp.float32)
    out = pl.pallas_call(
        functools.partial(correlate_kernel, first, depth, begun is not None, len(held)),
        out_shape=[product] + [jax.ShapeDtypeStruct(kept.shape, kept.dtype) for kept in held],
        in_specs=in_specs,
        out_specs=[WHOLE] + [ANYWHERE] * len(held),
        scratch_shapes=[pltpu.VMEM((2 * some, 2 * bands), jnp.float32)],
        input_output_aliases={before + index: 1 + index for index in range(len(held))},
        compiler_params=pltpu.CompilerParams(vmem_limit_bytes=16 * MIB),
        cost_estimate=pl.CostEstimate(flops=0, bytes_accessed=1024, transcendentals=0),
        name="correlate",
    )(*ins, *others, *held)
    return out if held else out[0]


def summed_over_pw(partial):
    pw = lax.axis_size("pw")
    if pw & (pw - 1):
        return partial + sum(moved(partial, "pw", d) for d in range(1, pw))
    distance = pw // 2
    while distance:
        partial = partial + lax.ppermute(partial, "pw", [(i, i ^ distance) for i in range(pw)])
        distance //= 2
    return partial


def sums_here_and_next(partial):
    ka, pw = lax.axis_size("ka"), lax.axis_size("pw")
    if pw & (pw - 1) or pw == 1:
        whole = summed_over_pw(partial)
        return [whole], [moved(whole, "ka", 1)]
    distance = pw // 2
    while distance > 1:
        partial = partial + lax.ppermute(partial, "pw", [(i, i ^ distance) for i in range(pw)])
        distance //= 2
    here = lax.ppermute(partial, "pw", [(i, i ^ 1) for i in range(pw)])
    across = [(k * pw + p, (k + 1) % ka * pw + (p ^ 1)) for k in range(ka) for p in range(pw)]
    before = [moved(partial, "ka", 1), lax.ppermute(partial, ("ka", "pw"), across)]
    return [partial, here], before


def assemble_kernel(counts, *refs):
    ins, (out_ref, made, sems) = list(refs[:-3]), refs[-3:]
    most, most_before, *last_refs = [[ins.pop(0) for _ in range(count)] for count in counts]
    copies = []
    for side in (1, 0):
        for c in (0, 1):
            early = [ref[c] for ref in (most, most_before)[side]]
            late = sum(ref[c] for ref in last_refs[side])
            matrix = jnp.concatenate([*early, late], axis=0)
            if side == 0:
                matrix = matrix.T
            elif c == 1:
                matrix = -matrix
            made[2 * side + c] = matrix
            copies.append(
                pltpu.make_async_copy(
                    made.at[2 * side + c], out_ref.at[0, side, c], sems.at[2 * side + c]
                )
            )
            copies[-1].start()
    for copy in copies:
        copy.wait()


def assembled(*parts):
    bands = parts[0][0].shape[2]
    counts = [len(part) for part in parts]
    return pl.pallas_call(
        functools.partial(assemble_kernel, counts),
        out_shape=jax.ShapeDtypeStruct((1, 2, 2, bands, bands), jnp.float32),
        in_specs=[WHOLE] * sum(counts),
        out_specs=ANYWHERE,
        scratch_shapes=[
            pltpu.VMEM((4, bands, bands), jnp.float32),
            pltpu.SemaphoreType.DMA((4,)),
        ],
        compiler_params=pltpu.CompilerParams(vmem_limit_bytes=16 * MIB),
        cost_estimate=pl.CostEstimate(flops=0, bytes_accessed=1024, transcendentals=0),
        name="assemble",
    )(*[array for part in parts for array in part])


def local(coefficients, shifts):
    bands, width = coefficients.shape[2:]
    unit = bands // sum(SIXTEENTHS)
    edges = [0]
    for size in SIXTEENTHS:
        edges.append(edges[-1] + size * unit)
    late = width // PWB * 3 // 4 * PWB
    coefficients = pltpu.with_memory_space_constraint(coefficients, pltpu.HBM)
    ranges = [(chunk, 0, width) for chunk in range(4)] + [(4, 0, late), (4, late, width)]
    blocks = []
    for chunk, low, high in ranges:
        some = slice(edges[chunk], edges[chunk + 1])
        blocks.append(cut(coefficients, some, slice(low, high), *blocks[-1:]))
    placed = placed_bands(coefficients, shifts, *blocks[-1:])
    placed = pltpu.with_memory_space_constraint(placed, pltpu.VMEM)
    arrived = [moved(block, "ka", -1) for block in blocks[:3]]
    whole = []
    for chunk in range(4):
        waiting = blocks[3 + chunk : 4 + chunk]
        partial = correlate(placed, arrived[chunk], *whole[-1:], held=waiting)
        if waiting:
            partial, waiting = partial
            arrived.append(moved(waiting, "ka", -1))
        whole.append(summed_over_pw(partial))
    most = jnp.concatenate(whole, axis=1)
    last, most = correlate(placed, arrived[4], held=[most])
    most_before = moved(most, "ka", 1)
    last = correlate(placed, arrived[5], first=late, begun=last)
    return assembled([most], [most_before], *sums_here_and_next(last))


def solution(mesh):
    return jax.shard_map(
        local,
        mesh=mesh,
        in_specs=(P(("groups", "ka"), None, None, "pw"), P(("groups", "ka"), None, "pw")),
        out_specs=P(("groups", "ka"), None, None, None, None),
        check_vma=False,
    )
```

```python
import functools

import jax
import jax.numpy as jnp
from jax import lax
from jax.experimental import pallas as pl
from jax.experimental.pallas import tpu as pltpu
from jax.sharding import PartitionSpec as P

PWB = 256
SIXTEENTHS = (2, 6, 4, 2, 2)
MIB = 1 << 20
PLACE_FLOPS = 1 << 36
ANYWHERE = pl.BlockSpec(memory_space=pl.ANY)
WHOLE = pl.BlockSpec(memory_space=pltpu.VMEM)


def moved(block, axis, distance):
    count = lax.axis_size(axis)
    return lax.ppermute(block, axis, [(i, (i + distance) % count) for i in range(count)])


def cut_kernel(bands, waves, *refs):
    own_ref, out_ref, sems = refs[0], refs[-2], refs[-1]
    copies = [
        pltpu.make_async_copy(own_ref.at[0, c, bands, waves], out_ref.at[c], sems.at[c])
        for c in range(2)
    ]
    for copy in copies:
        copy.start()
    for copy in copies:
        copy.wait()


def cut(coefficients, bands, waves, *others):
    shape = (2, bands.stop - bands.start, waves.stop - waves.start)
    return pl.pallas_call(
        functools.partial(cut_kernel, bands, waves),
        out_shape=jax.ShapeDtypeStruct(shape, coefficients.dtype),
        in_specs=[ANYWHERE] * (1 + len(others)),
        out_specs=ANYWHERE,
        scratch_shapes=[pltpu.SemaphoreType.DMA((2,))],
        compiler_params=pltpu.CompilerParams(vmem_limit_bytes=MIB),
        cost_estimate=pl.CostEstimate(flops=0, bytes_accessed=1024, transcendentals=0),
        name="cut",
    )(coefficients, *others)


def place_kernel(own_ref, shift_ref, *refs):
    out_ref = refs[-1]
    bands, width = own_ref.shape[2:]
    base = pl.program_id(0) * width
    goal = lax.broadcasted_iota(jnp.int32, (PWB, PWB), 0)
    for block in range(width // PWB):
        here = pl.ds(block * PWB, PWB)
        inside = shift_ref[0, 0:1, here] & (PWB - 1)
        selector = (goal == inside).astype(jnp.float32).astype(jnp.bfloat16)
        rows = own_ref[0, :, :, here].reshape(2 * bands, PWB)
        placed = lax.dot_general(
            selector, rows, (((1,), (1,)), ((), ())), preferred_element_type=jnp.float32
        )
        there = pl.multiple_of(base + block * PWB, PWB)
        out_ref[pl.ds(there, PWB), :] = placed.astype(jnp.bfloat16)


def placed_bands(coefficients, shifts, *others):
    bands, width = coefficients.shape[2:]
    step = 4 * PWB if width % (4 * PWB) == 0 else PWB
    return pl.pallas_call(
        place_kernel,
        grid=(width // step,),
        out_shape=pltpu.VMEM((width, 2 * bands), jnp.bfloat16),
        in_specs=[
            pl.BlockSpec((1, 2, bands, step), lambda g: (0, 0, 0, g)),
            pl.BlockSpec((1, 2, step), lambda g: (0, 0, g)),
        ]
        + [ANYWHERE] * len(others),
        out_specs=WHOLE,
        compiler_params=pltpu.CompilerParams(vmem_limit_bytes=16 * MIB),
        cost_estimate=pl.CostEstimate(flops=PLACE_FLOPS, bytes_accessed=1024, transcendentals=0),
        name="place",
    )(coefficients, shifts, *others)


def correlate_kernel(first, depth, begun, held, placed_ref, block_ref, *refs):
    out_ref, total = refs[-2 - held], refs[-1]
    some, width = block_ref.shape[1:]
    bands = out_ref.shape[2]

    def product_of(start):
        return jnp.dot(
            block_ref[:, :, pl.ds(start, depth)].reshape(2 * some, depth),
            placed_ref[pl.ds(first + start, depth), :],
            preferred_element_type=jnp.float32,
        )

    total[...] = product_of(0)

    @pl.loop(1, width // depth)
    def _(step):
        total[...] += product_of(pl.multiple_of(step * depth, depth))

    real_part = total[:some, :bands] + total[some:, bands:]
    imag_part = total[some:, :bands] - total[:some, bands:]
    out_ref[0] = refs[0][0] + real_part if begun else real_part
    out_ref[1] = refs[0][1] + imag_part if begun else imag_part


def correlate(placed, block, *others, first=0, begun=None, held=()):
    some, width = block.shape[1:]
    bands = placed.shape[1] // 2
    depth = width
    while depth % (2 * PWB) == 0 and some * depth > 1 << 19:
        depth //= 2
    block = pltpu.with_memory_space_constraint(block, pltpu.VMEM)
    ins = [placed, block] if begun is None else [placed, block, begun]
    in_specs = [WHOLE] * len(ins) + [ANYWHERE] * (len(others) + len(held))
    before = len(ins) + len(others)
    product = jax.ShapeDtypeStruct((2, some, bands), jnp.float32)
    out = pl.pallas_call(
        functools.partial(correlate_kernel, first, depth, begun is not None, len(held)),
        out_shape=[product] + [jax.ShapeDtypeStruct(kept.shape, kept.dtype) for kept in held],
        in_specs=in_specs,
        out_specs=[WHOLE] + [ANYWHERE] * len(held),
        scratch_shapes=[pltpu.VMEM((2 * some, 2 * bands), jnp.float32)],
        input_output_aliases={before + index: 1 + index for index in range(len(held))},
        compiler_params=pltpu.CompilerParams(vmem_limit_bytes=16 * MIB),
        cost_estimate=pl.CostEstimate(flops=0, bytes_accessed=1024, transcendentals=0),
        name="correlate",
    )(*ins, *others, *held)
    return out if held else out[0]


def summed_over_pw(partial):
    pw = lax.axis_size("pw")
    if pw & (pw - 1):
        return partial + sum(moved(partial, "pw", d) for d in range(1, pw))
    distance = pw // 2
    while distance:
        partial = partial + lax.ppermute(partial, "pw", [(i, i ^ distance) for i in range(pw)])
        distance //= 2
    return partial


def sums_here_and_next(partial):
    ka, pw = lax.axis_size("ka"), lax.axis_size("pw")
    if pw & (pw - 1) or pw == 1:
        whole = summed_over_pw(partial)
        return [whole], [moved(whole, "ka", 1)]
    distance = pw // 2
    while distance > 1:
        partial = partial + lax.ppermute(partial, "pw", [(i, i ^ distance) for i in range(pw)])
        distance //= 2
    here = lax.ppermute(partial, "pw", [(i, i ^ 1) for i in range(pw)])
    across = [(k * pw + p, (k + 1) % ka * pw + (p ^ 1)) for k in range(ka) for p in range(pw)]
    before = [moved(partial, "ka", 1), lax.ppermute(partial, ("ka", "pw"), across)]
    return [partial, here], before


def assemble_kernel(counts, *refs):
    ins, (out_ref, made, sems) = list(refs[:-3]), refs[-3:]
    most, most_before, *last_refs = [[ins.pop(0) for _ in range(count)] for count in counts]
    copies = []
    for side in (1, 0):
        for c in (0, 1):
            early = [ref[c] for ref in (most, most_before)[side]]
            late = sum(ref[c] for ref in last_refs[side])
            matrix = jnp.concatenate([*early, late], axis=0)
            if side == 0:
                matrix = matrix.T
            elif c == 1:
                matrix = -matrix
            made[2 * side + c] = matrix
            copies.append(
                pltpu.make_async_copy(
                    made.at[2 * side + c], out_ref.at[0, side, c], sems.at[2 * side + c]
                )
            )
            copies[-1].start()
    for copy in copies:
        copy.wait()


def assembled(*parts):
    bands = parts[0][0].shape[2]
    counts = [len(part) for part in parts]
    return pl.pallas_call(
        functools.partial(assemble_kernel, counts),
        out_shape=jax.ShapeDtypeStruct((1, 2, 2, bands, bands), jnp.float32),
        in_specs=[WHOLE] * sum(counts),
        out_specs=ANYWHERE,
        scratch_shapes=[
            pltpu.VMEM((4, bands, bands), jnp.float32),
            pltpu.SemaphoreType.DMA((4,)),
        ],
        compiler_params=pltpu.CompilerParams(vmem_limit_bytes=16 * MIB),
        cost_estimate=pl.CostEstimate(flops=0, bytes_accessed=1024, transcendentals=0),
        name="assemble",
    )(*[array for part in parts for array in part])


def local(coefficients, shifts):
    bands, width = coefficients.shape[2:]
    unit = bands // sum(SIXTEENTHS)
    edges = [0]
    for size in SIXTEENTHS:
        edges.append(edges[-1] + size * unit)
    late = width // PWB * 3 // 4 * PWB
    coefficients = pltpu.with_memory_space_constraint(coefficients, pltpu.HBM)
    ranges = [(chunk, 0, width) for chunk in range(4)] + [(4, 0, late), (4, late, width)]
    blocks = []
    for chunk, low, high in ranges:
        some = slice(edges[chunk], edges[chunk + 1])
        blocks.append(cut(coefficients, some, slice(low, high), *blocks[-1:]))
    placed = placed_bands(coefficients, shifts, *blocks[-1:])
    placed = pltpu.with_memory_space_constraint(placed, pltpu.VMEM)
    arrived = [moved(block, "ka", -1) for block in blocks[:3]]
    whole = []
    for chunk in range(4):
        waiting = blocks[2 + chunk : 3 + chunk] if chunk else []
        partial = correlate(placed, arrived[chunk], *whole[-1:], held=waiting)
        if waiting:
            partial, waiting = partial
            arrived.append(moved(waiting, "ka", -1))
        whole.append(summed_over_pw(partial))
    most = jnp.concatenate(whole, axis=1)
    last, most = correlate(placed, arrived[4], held=[most])
    most_before = moved(most, "ka", 1)
    last = correlate(placed, arrived[5], first=late, begun=last)
    return assembled([most], [most_before], *sums_here_and_next(last))


def solution(mesh):
    return jax.shard_map(
        local,
        mesh=mesh,
        in_specs=(P(("groups", "ka"), None, None, "pw"), P(("groups", "ka"), None, "pw")),
        out_specs=P(("groups", "ka"), None, None, None, None),
        check_vma=False,
    )
```

```python
import functools

import jax
import jax.numpy as jnp
from jax import lax
from jax.experimental import pallas as pl
from jax.experimental.pallas import tpu as pltpu
from jax.sharding import PartitionSpec as P

PWB = 256
SIXTEENTHS = (2, 7, 3, 2, 2)
MIB = 1 << 20
PLACE_FLOPS = 1 << 36
ANYWHERE = pl.BlockSpec(memory_space=pl.ANY)
WHOLE = pl.BlockSpec(memory_space=pltpu.VMEM)


def moved(block, axis, distance):
    count = lax.axis_size(axis)
    return lax.ppermute(block, axis, [(i, (i + distance) % count) for i in range(count)])


def cut_kernel(bands, waves, *refs):
    own_ref, out_ref, sems = refs[0], refs[-2], refs[-1]
    copies = [
        pltpu.make_async_copy(own_ref.at[0, c, bands, waves], out_ref.at[c], sems.at[c])
        for c in range(2)
    ]
    for copy in copies:
        copy.start()
    for copy in copies:
        copy.wait()


def cut(coefficients, bands, waves, *others):
    shape = (2, bands.stop - bands.start, waves.stop - waves.start)
    return pl.pallas_call(
        functools.partial(cut_kernel, bands, waves),
        out_shape=jax.ShapeDtypeStruct(shape, coefficients.dtype),
        in_specs=[ANYWHERE] * (1 + len(others)),
        out_specs=ANYWHERE,
        scratch_shapes=[pltpu.SemaphoreType.DMA((2,))],
        compiler_params=pltpu.CompilerParams(vmem_limit_bytes=MIB),
        cost_estimate=pl.CostEstimate(flops=0, bytes_accessed=1024, transcendentals=0),
        name="cut",
    )(coefficients, *others)


def place_kernel(own_ref, shift_ref, *refs):
    out_ref = refs[-1]
    bands, width = own_ref.shape[2:]
    base = pl.program_id(0) * width
    goal = lax.broadcasted_iota(jnp.int32, (PWB, PWB), 0)
    for block in range(width // PWB):
        here = pl.ds(block * PWB, PWB)
        inside = shift_ref[0, 0:1, here] & (PWB - 1)
        selector = (goal == inside).astype(jnp.float32).astype(jnp.bfloat16)
        rows = own_ref[0, :, :, here].reshape(2 * bands, PWB)
        placed = lax.dot_general(
            selector, rows, (((1,), (1,)), ((), ())), preferred_element_type=jnp.float32
        )
        there = pl.multiple_of(base + block * PWB, PWB)
        out_ref[pl.ds(there, PWB), :] = placed.astype(jnp.bfloat16)


def placed_bands(coefficients, shifts, *others):
    bands, width = coefficients.shape[2:]
    step = 4 * PWB if width % (4 * PWB) == 0 else PWB
    return pl.pallas_call(
        place_kernel,
        grid=(width // step,),
        out_shape=pltpu.VMEM((width, 2 * bands), jnp.bfloat16),
        in_specs=[
            pl.BlockSpec((1, 2, bands, step), lambda g: (0, 0, 0, g)),
            pl.BlockSpec((1, 2, step), lambda g: (0, 0, g)),
        ]
        + [ANYWHERE] * len(others),
        out_specs=WHOLE,
        compiler_params=pltpu.CompilerParams(vmem_limit_bytes=16 * MIB),
        cost_estimate=pl.CostEstimate(flops=PLACE_FLOPS, bytes_accessed=1024, transcendentals=0),
        name="place",
    )(coefficients, shifts, *others)


def correlate_kernel(first, depth, begun, held, placed_ref, block_ref, *refs):
    out_ref, total = refs[-2 - held], refs[-1]
    some, width = block_ref.shape[1:]
    bands = out_ref.shape[2]

    def product_of(start):
        return jnp.dot(
            block_ref[:, :, pl.ds(start, depth)].reshape(2 * some, depth),
            placed_ref[pl.ds(first + start, depth), :],
            preferred_element_type=jnp.float32,
        )

    total[...] = product_of(0)

    @pl.loop(1, width // depth)
    def _(step):
        total[...] += product_of(pl.multiple_of(step * depth, depth))

    real_part = total[:some, :bands] + total[some:, bands:]
    imag_part = total[some:, :bands] - total[:some, bands:]
    out_ref[0] = refs[0][0] + real_part if begun else real_part
    out_ref[1] = refs[0][1] + imag_part if begun else imag_part


def correlate(placed, block, *others, first=0, begun=None, held=()):
    some, width = block.shape[1:]
    bands = placed.shape[1] // 2
    depth = width
    while depth % (2 * PWB) == 0 and some * depth > 1 << 19:
        depth //= 2
    block = pltpu.with_memory_space_constraint(block, pltpu.VMEM)
    ins = [placed, block] if begun is None else [placed, block, begun]
    in_specs = [WHOLE] * len(ins) + [ANYWHERE] * (len(others) + len(held))
    before = len(ins) + len(others)
    product = jax.ShapeDtypeStruct((2, some, bands), jnp.float32)
    out = pl.pallas_call(
        functools.partial(correlate_kernel, first, depth, begun is not None, len(held)),
        out_shape=[product] + [jax.ShapeDtypeStruct(kept.shape, kept.dtype) for kept in held],
        in_specs=in_specs,
        out_specs=[WHOLE] + [ANYWHERE] * len(held),
        scratch_shapes=[pltpu.VMEM((2 * some, 2 * bands), jnp.float32)],
        input_output_aliases={before + index: 1 + index for index in range(len(held))},
        compiler_params=pltpu.CompilerParams(vmem_limit_bytes=16 * MIB),
        cost_estimate=pl.CostEstimate(flops=0, bytes_accessed=1024, transcendentals=0),
        name="correlate",
    )(*ins, *others, *held)
    return out if held else out[0]


def summed_over_pw(partial):
    pw = lax.axis_size("pw")
    if pw & (pw - 1):
        return partial + sum(moved(partial, "pw", d) for d in range(1, pw))
    distance = pw // 2
    while distance:
        partial = partial + lax.ppermute(partial, "pw", [(i, i ^ distance) for i in range(pw)])
        distance //= 2
    return partial


def sums_here_and_next(partial):
    ka, pw = lax.axis_size("ka"), lax.axis_size("pw")
    if pw & (pw - 1) or pw == 1:
        whole = summed_over_pw(partial)
        return [whole], [moved(whole, "ka", 1)]
    distance = pw // 2
    while distance > 1:
        partial = partial + lax.ppermute(partial, "pw", [(i, i ^ distance) for i in range(pw)])
        distance //= 2
    here = lax.ppermute(partial, "pw", [(i, i ^ 1) for i in range(pw)])
    across = [(k * pw + p, (k + 1) % ka * pw + (p ^ 1)) for k in range(ka) for p in range(pw)]
    before = [moved(partial, "ka", 1), lax.ppermute(partial, ("ka", "pw"), across)]
    return [partial, here], before


def assemble_kernel(counts, *refs):
    ins, (out_ref, made, sems) = list(refs[:-3]), refs[-3:]
    most, most_before, *last_refs = [[ins.pop(0) for _ in range(count)] for count in counts]
    copies = []
    for side in (1, 0):
        for c in (0, 1):
            early = [ref[c] for ref in (most, most_before)[side]]
            late = sum(ref[c] for ref in last_refs[side])
            matrix = jnp.concatenate([*early, late], axis=0)
            if side == 0:
                matrix = matrix.T
            elif c == 1:
                matrix = -matrix
            made[2 * side + c] = matrix
            copies.append(
                pltpu.make_async_copy(
                    made.at[2 * side + c], out_ref.at[0, side, c], sems.at[2 * side + c]
                )
            )
            copies[-1].start()
    for copy in copies:
        copy.wait()


def assembled(*parts):
    bands = parts[0][0].shape[2]
    counts = [len(part) for part in parts]
    return pl.pallas_call(
        functools.partial(assemble_kernel, counts),
        out_shape=jax.ShapeDtypeStruct((1, 2, 2, bands, bands), jnp.float32),
        in_specs=[WHOLE] * sum(counts),
        out_specs=ANYWHERE,
        scratch_shapes=[
            pltpu.VMEM((4, bands, bands), jnp.float32),
            pltpu.SemaphoreType.DMA((4,)),
        ],
        compiler_params=pltpu.CompilerParams(vmem_limit_bytes=16 * MIB),
        cost_estimate=pl.CostEstimate(flops=0, bytes_accessed=1024, transcendentals=0),
        name="assemble",
    )(*[array for part in parts for array in part])


def local(coefficients, shifts):
    bands, width = coefficients.shape[2:]
    unit = bands // sum(SIXTEENTHS)
    edges = [0]
    for size in SIXTEENTHS:
        edges.append(edges[-1] + size * unit)
    late = width // PWB * 3 // 4 * PWB
    coefficients = pltpu.with_memory_space_constraint(coefficients, pltpu.HBM)
    ranges = [(chunk, 0, width) for chunk in range(4)] + [(4, 0, late), (4, late, width)]
    blocks = []
    for chunk, low, high in ranges:
        some = slice(edges[chunk], edges[chunk + 1])
        blocks.append(cut(coefficients, some, slice(low, high), *blocks[-1:]))
    placed = placed_bands(coefficients, shifts, *blocks[-1:])
    placed = pltpu.with_memory_space_constraint(placed, pltpu.VMEM)
    arrived = [moved(block, "ka", -1) for block in blocks[:3]]
    whole = []
    for chunk in range(4):
        waiting = blocks[2 + chunk : 3 + chunk] if chunk else []
        partial = correlate(placed, arrived[chunk], *whole[-1:], held=waiting)
        if waiting:
            partial, waiting = partial
            arrived.append(moved(waiting, "ka", -1))
        whole.append(summed_over_pw(partial))
    most = jnp.concatenate(whole, axis=1)
    last, most = correlate(placed, arrived[4], held=[most])
    most_before = moved(most, "ka", 1)
    last = correlate(placed, arrived[5], first=late, begun=last)
    return assembled([most], [most_before], *sums_here_and_next(last))


def solution(mesh):
    return jax.shard_map(
        local,
        mesh=mesh,
        in_specs=(P(("groups", "ka"), None, None, "pw"), P(("groups", "ka"), None, "pw")),
        out_specs=P(("groups", "ka"), None, None, None, None),
        check_vma=False,
    )
```

```python
import functools

import jax
import jax.numpy as jnp
from jax import lax
from jax.experimental import pallas as pl
from jax.experimental.pallas import tpu as pltpu
from jax.sharding import PartitionSpec as P

PWB = 256
SIXTEENTHS = (2, 5, 3, 2, 2, 2)
MIB = 1 << 20
PLACE_FLOPS = 1 << 36
ANYWHERE = pl.BlockSpec(memory_space=pl.ANY)
WHOLE = pl.BlockSpec(memory_space=pltpu.VMEM)


def moved(block, axis, distance):
    count = lax.axis_size(axis)
    return lax.ppermute(block, axis, [(i, (i + distance) % count) for i in range(count)])


def cut_kernel(bands, waves, *refs):
    own_ref, out_ref, sems = refs[0], refs[-2], refs[-1]
    copies = [
        pltpu.make_async_copy(own_ref.at[0, c, bands, waves], out_ref.at[c], sems.at[c])
        for c in range(2)
    ]
    for copy in copies:
        copy.start()
    for copy in copies:
        copy.wait()


def cut(coefficients, bands, waves, *others):
    shape = (2, bands.stop - bands.start, waves.stop - waves.start)
    return pl.pallas_call(
        functools.partial(cut_kernel, bands, waves),
        out_shape=jax.ShapeDtypeStruct(shape, coefficients.dtype),
        in_specs=[ANYWHERE] * (1 + len(others)),
        out_specs=ANYWHERE,
        scratch_shapes=[pltpu.SemaphoreType.DMA((2,))],
        compiler_params=pltpu.CompilerParams(vmem_limit_bytes=MIB),
        cost_estimate=pl.CostEstimate(flops=0, bytes_accessed=1024, transcendentals=0),
        name="cut",
    )(coefficients, *others)


def place_kernel(own_ref, shift_ref, *refs):
    out_ref = refs[-1]
    bands, width = own_ref.shape[2:]
    base = pl.program_id(0) * width
    goal = lax.broadcasted_iota(jnp.int32, (PWB, PWB), 0)
    for block in range(width // PWB):
        here = pl.ds(block * PWB, PWB)
        inside = shift_ref[0, 0:1, here] & (PWB - 1)
        selector = (goal == inside).astype(jnp.float32).astype(jnp.bfloat16)
        rows = own_ref[0, :, :, here].reshape(2 * bands, PWB)
        placed = lax.dot_general(
            selector, rows, (((1,), (1,)), ((), ())), preferred_element_type=jnp.float32
        )
        there = pl.multiple_of(base + block * PWB, PWB)
        out_ref[pl.ds(there, PWB), :] = placed.astype(jnp.bfloat16)


def placed_bands(coefficients, shifts, *others):
    bands, width = coefficients.shape[2:]
    step = 4 * PWB if width % (4 * PWB) == 0 else PWB
    return pl.pallas_call(
        place_kernel,
        grid=(width // step,),
        out_shape=pltpu.VMEM((width, 2 * bands), jnp.bfloat16),
        in_specs=[
            pl.BlockSpec((1, 2, bands, step), lambda g: (0, 0, 0, g)),
            pl.BlockSpec((1, 2, step), lambda g: (0, 0, g)),
        ]
        + [ANYWHERE] * len(others),
        out_specs=WHOLE,
        compiler_params=pltpu.CompilerParams(vmem_limit_bytes=16 * MIB),
        cost_estimate=pl.CostEstimate(flops=PLACE_FLOPS, bytes_accessed=1024, transcendentals=0),
        name="place",
    )(coefficients, shifts, *others)


def correlate_kernel(first, depth, begun, held, placed_ref, block_ref, *refs):
    out_ref, total = refs[-2 - held], refs[-1]
    some, width = block_ref.shape[1:]
    bands = out_ref.shape[2]

    def product_of(start):
        return jnp.dot(
            block_ref[:, :, pl.ds(start, depth)].reshape(2 * some, depth),
            placed_ref[pl.ds(first + start, depth), :],
            preferred_element_type=jnp.float32,
        )

    total[...] = product_of(0)

    @pl.loop(1, width // depth)
    def _(step):
        total[...] += product_of(pl.multiple_of(step * depth, depth))

    real_part = total[:some, :bands] + total[some:, bands:]
    imag_part = total[some:, :bands] - total[:some, bands:]
    out_ref[0] = refs[0][0] + real_part if begun else real_part
    out_ref[1] = refs[0][1] + imag_part if begun else imag_part


def correlate(placed, block, *others, first=0, begun=None, held=()):
    some, width = block.shape[1:]
    bands = placed.shape[1] // 2
    depth = width
    while depth % (2 * PWB) == 0 and some * depth > 1 << 19:
        depth //= 2
    block = pltpu.with_memory_space_constraint(block, pltpu.VMEM)
    ins = [placed, block] if begun is None else [placed, block, begun]
    in_specs = [WHOLE] * len(ins) + [ANYWHERE] * (len(others) + len(held))
    before = len(ins) + len(others)
    product = jax.ShapeDtypeStruct((2, some, bands), jnp.float32)
    out = pl.pallas_call(
        functools.partial(correlate_kernel, first, depth, begun is not None, len(held)),
        out_shape=[product] + [jax.ShapeDtypeStruct(kept.shape, kept.dtype) for kept in held],
        in_specs=in_specs,
        out_specs=[WHOLE] + [ANYWHERE] * len(held),
        scratch_shapes=[pltpu.VMEM((2 * some, 2 * bands), jnp.float32)],
        input_output_aliases={before + index: 1 + index for index in range(len(held))},
        compiler_params=pltpu.CompilerParams(vmem_limit_bytes=16 * MIB),
        cost_estimate=pl.CostEstimate(flops=0, bytes_accessed=1024, transcendentals=0),
        name="correlate",
    )(*ins, *others, *held)
    return out if held else out[0]


def summed_over_pw(partial):
    pw = lax.axis_size("pw")
    if pw & (pw - 1):
        return partial + sum(moved(partial, "pw", d) for d in range(1, pw))
    distance = pw // 2
    while distance:
        partial = partial + lax.ppermute(partial, "pw", [(i, i ^ distance) for i in range(pw)])
        distance //= 2
    return partial


def sums_here_and_next(partial):
    ka, pw = lax.axis_size("ka"), lax.axis_size("pw")
    if pw & (pw - 1) or pw == 1:
        whole = summed_over_pw(partial)
        return [whole], [moved(whole, "ka", 1)]
    distance = pw // 2
    while distance > 1:
        partial = partial + lax.ppermute(partial, "pw", [(i, i ^ distance) for i in range(pw)])
        distance //= 2
    here = lax.ppermute(partial, "pw", [(i, i ^ 1) for i in range(pw)])
    across = [(k * pw + p, (k + 1) % ka * pw + (p ^ 1)) for k in range(ka) for p in range(pw)]
    before = [moved(partial, "ka", 1), lax.ppermute(partial, ("ka", "pw"), across)]
    return [partial, here], before


def assemble_kernel(counts, *refs):
    ins, (out_ref, made, sems) = list(refs[:-3]), refs[-3:]
    most, most_before, *last_refs = [[ins.pop(0) for _ in range(count)] for count in counts]
    copies = []
    for side in (1, 0):
        for c in (0, 1):
            early = [ref[c] for ref in (most, most_before)[side]]
            late = sum(ref[c] for ref in last_refs[side])
            matrix = jnp.concatenate([*early, late], axis=0)
            if side == 0:
                matrix = matrix.T
            elif c == 1:
                matrix = -matrix
            made[2 * side + c] = matrix
            copies.append(
                pltpu.make_async_copy(
                    made.at[2 * side + c], out_ref.at[0, side, c], sems.at[2 * side + c]
                )
            )
            copies[-1].start()
    for copy in copies:
        copy.wait()


def assembled(*parts):
    bands = parts[0][0].shape[2]
    counts = [len(part) for part in parts]
    return pl.pallas_call(
        functools.partial(assemble_kernel, counts),
        out_shape=jax.ShapeDtypeStruct((1, 2, 2, bands, bands), jnp.float32),
        in_specs=[WHOLE] * sum(counts),
        out_specs=ANYWHERE,
        scratch_shapes=[
            pltpu.VMEM((4, bands, bands), jnp.float32),
            pltpu.SemaphoreType.DMA((4,)),
        ],
        compiler_params=pltpu.CompilerParams(vmem_limit_bytes=16 * MIB),
        cost_estimate=pl.CostEstimate(flops=0, bytes_accessed=1024, transcendentals=0),
        name="assemble",
    )(*[array for part in parts for array in part])


def local(coefficients, shifts):
    bands, width = coefficients.shape[2:]
    unit = bands // sum(SIXTEENTHS)
    edges = [0]
    for size in SIXTEENTHS:
        edges.append(edges[-1] + size * unit)
    late = width // PWB * 3 // 4 * PWB
    coefficients = pltpu.with_memory_space_constraint(coefficients, pltpu.HBM)
    ranges = [(chunk, 0, width) for chunk in range(5)] + [(5, 0, late), (5, late, width)]
    blocks = []
    for chunk, low, high in ranges:
        some = slice(edges[chunk], edges[chunk + 1])
        blocks.append(cut(coefficients, some, slice(low, high), *blocks[-1:]))
    placed = placed_bands(coefficients, shifts, *blocks[-1:])
    placed = pltpu.with_memory_space_constraint(placed, pltpu.VMEM)
    arrived = [moved(block, "ka", -1) for block in blocks[:3]]
    whole = []
    for chunk in range(5):
        waiting = blocks[2 + chunk : 3 + chunk] if chunk else []
        partial = correlate(placed, arrived[chunk], *whole[-1:], held=waiting)
        if waiting:
            partial, waiting = partial
            arrived.append(moved(waiting, "ka", -1))
        whole.append(summed_over_pw(partial))
    most = jnp.concatenate(whole, axis=1)
    last, most = correlate(placed, arrived[5], held=[most])
    most_before = moved(most, "ka", 1)
    last = correlate(placed, arrived[6], first=late, begun=last)
    return assembled([most], [most_before], *sums_here_and_next(last))


def solution(mesh):
    return jax.shard_map(
        local,
        mesh=mesh,
        in_specs=(P(("groups", "ka"), None, None, "pw"), P(("groups", "ka"), None, "pw")),
        out_specs=P(("groups", "ka"), None, None, None, None),
        check_vma=False,
    )
```

```python
import functools

import jax
import jax.numpy as jnp
from jax import lax
from jax.experimental import pallas as pl
from jax.experimental.pallas import tpu as pltpu
from jax.sharding import PartitionSpec as P

PWB = 256
SIXTEENTHS = (1, 6, 3, 2, 2, 2)
MIB = 1 << 20
PLACE_FLOPS = 1 << 36
ANYWHERE = pl.BlockSpec(memory_space=pl.ANY)
WHOLE = pl.BlockSpec(memory_space=pltpu.VMEM)


def moved(block, axis, distance):
    count = lax.axis_size(axis)
    return lax.ppermute(block, axis, [(i, (i + distance) % count) for i in range(count)])


def cut_kernel(bands, waves, *refs):
    own_ref, out_ref, sems = refs[0], refs[-2], refs[-1]
    copies = [
        pltpu.make_async_copy(own_ref.at[0, c, bands, waves], out_ref.at[c], sems.at[c])
        for c in range(2)
    ]
    for copy in copies:
        copy.start()
    for copy in copies:
        copy.wait()


def cut(coefficients, bands, waves, *others):
    shape = (2, bands.stop - bands.start, waves.stop - waves.start)
    return pl.pallas_call(
        functools.partial(cut_kernel, bands, waves),
        out_shape=jax.ShapeDtypeStruct(shape, coefficients.dtype),
        in_specs=[ANYWHERE] * (1 + len(others)),
        out_specs=ANYWHERE,
        scratch_shapes=[pltpu.SemaphoreType.DMA((2,))],
        compiler_params=pltpu.CompilerParams(vmem_limit_bytes=MIB),
        cost_estimate=pl.CostEstimate(flops=0, bytes_accessed=1024, transcendentals=0),
        name="cut",
    )(coefficients, *others)


def place_kernel(own_ref, shift_ref, *refs):
    out_ref = refs[-1]
    bands, width = own_ref.shape[2:]
    base = pl.program_id(0) * width
    goal = lax.broadcasted_iota(jnp.int32, (PWB, PWB), 0)
    for block in range(width // PWB):
        here = pl.ds(block * PWB, PWB)
        inside = shift_ref[0, 0:1, here] & (PWB - 1)
        selector = (goal == inside).astype(jnp.float32).astype(jnp.bfloat16)
        rows = own_ref[0, :, :, here].reshape(2 * bands, PWB)
        placed = lax.dot_general(
            selector, rows, (((1,), (1,)), ((), ())), preferred_element_type=jnp.float32
        )
        there = pl.multiple_of(base + block * PWB, PWB)
        out_ref[pl.ds(there, PWB), :] = placed.astype(jnp.bfloat16)


def placed_bands(coefficients, shifts, *others):
    bands, width = coefficients.shape[2:]
    step = 4 * PWB if width % (4 * PWB) == 0 else PWB
    return pl.pallas_call(
        place_kernel,
        grid=(width // step,),
        out_shape=pltpu.VMEM((width, 2 * bands), jnp.bfloat16),
        in_specs=[
            pl.BlockSpec((1, 2, bands, step), lambda g: (0, 0, 0, g)),
            pl.BlockSpec((1, 2, step), lambda g: (0, 0, g)),
        ]
        + [ANYWHERE] * len(others),
        out_specs=WHOLE,
        compiler_params=pltpu.CompilerParams(vmem_limit_bytes=16 * MIB),
        cost_estimate=pl.CostEstimate(flops=PLACE_FLOPS, bytes_accessed=1024, transcendentals=0),
        name="place",
    )(coefficients, shifts, *others)


def correlate_kernel(first, depth, begun, held, placed_ref, block_ref, *refs):
    out_ref, total = refs[-2 - held], refs[-1]
    some, width = block_ref.shape[1:]
    bands = out_ref.shape[2]

    def product_of(start):
        return jnp.dot(
            block_ref[:, :, pl.ds(start, depth)].reshape(2 * some, depth),
            placed_ref[pl.ds(first + start, depth), :],
            preferred_element_type=jnp.float32,
        )

    total[...] = product_of(0)

    @pl.loop(1, width // depth)
    def _(step):
        total[...] += product_of(pl.multiple_of(step * depth, depth))

    real_part = total[:some, :bands] + total[some:, bands:]
    imag_part = total[some:, :bands] - total[:some, bands:]
    out_ref[0] = refs[0][0] + real_part if begun else real_part
    out_ref[1] = refs[0][1] + imag_part if begun else imag_part


def correlate(placed, block, *others, first=0, begun=None, held=()):
    some, width = block.shape[1:]
    bands = placed.shape[1] // 2
    depth = width
    while depth % (2 * PWB) == 0 and some * depth > 1 << 19:
        depth //= 2
    block = pltpu.with_memory_space_constraint(block, pltpu.VMEM)
    ins = [placed, block] if begun is None else [placed, block, begun]
    in_specs = [WHOLE] * len(ins) + [ANYWHERE] * (len(others) + len(held))
    before = len(ins) + len(others)
    product = jax.ShapeDtypeStruct((2, some, bands), jnp.float32)
    out = pl.pallas_call(
        functools.partial(correlate_kernel, first, depth, begun is not None, len(held)),
        out_shape=[product] + [jax.ShapeDtypeStruct(kept.shape, kept.dtype) for kept in held],
        in_specs=in_specs,
        out_specs=[WHOLE] + [ANYWHERE] * len(held),
        scratch_shapes=[pltpu.VMEM((2 * some, 2 * bands), jnp.float32)],
        input_output_aliases={before + index: 1 + index for index in range(len(held))},
        compiler_params=pltpu.CompilerParams(vmem_limit_bytes=16 * MIB),
        cost_estimate=pl.CostEstimate(flops=0, bytes_accessed=1024, transcendentals=0),
        name="correlate",
    )(*ins, *others, *held)
    return out if held else out[0]


def summed_over_pw(partial):
    pw = lax.axis_size("pw")
    if pw & (pw - 1):
        return partial + sum(moved(partial, "pw", d) for d in range(1, pw))
    distance = pw // 2
    while distance:
        partial = partial + lax.ppermute(partial, "pw", [(i, i ^ distance) for i in range(pw)])
        distance //= 2
    return partial


def sums_here_and_next(partial):
    ka, pw = lax.axis_size("ka"), lax.axis_size("pw")
    if pw & (pw - 1) or pw == 1:
        whole = summed_over_pw(partial)
        return [whole], [moved(whole, "ka", 1)]
    distance = pw // 2
    while distance > 1:
        partial = partial + lax.ppermute(partial, "pw", [(i, i ^ distance) for i in range(pw)])
        distance //= 2
    here = lax.ppermute(partial, "pw", [(i, i ^ 1) for i in range(pw)])
    across = [(k * pw + p, (k + 1) % ka * pw + (p ^ 1)) for k in range(ka) for p in range(pw)]
    before = [moved(partial, "ka", 1), lax.ppermute(partial, ("ka", "pw"), across)]
    return [partial, here], before


def assemble_kernel(counts, *refs):
    ins, (out_ref, made, sems) = list(refs[:-3]), refs[-3:]
    most, most_before, *last_refs = [[ins.pop(0) for _ in range(count)] for count in counts]
    copies = []
    for side in (1, 0):
        for c in (0, 1):
            early = [ref[c] for ref in (most, most_before)[side]]
            late = sum(ref[c] for ref in last_refs[side])
            matrix = jnp.concatenate([*early, late], axis=0)
            if side == 0:
                matrix = matrix.T
            elif c == 1:
                matrix = -matrix
            made[2 * side + c] = matrix
            copies.append(
                pltpu.make_async_copy(
                    made.at[2 * side + c], out_ref.at[0, side, c], sems.at[2 * side + c]
                )
            )
            copies[-1].start()
    for copy in copies:
        copy.wait()


def assembled(*parts):
    bands = parts[0][0].shape[2]
    counts = [len(part) for part in parts]
    return pl.pallas_call(
        functools.partial(assemble_kernel, counts),
        out_shape=jax.ShapeDtypeStruct((1, 2, 2, bands, bands), jnp.float32),
        in_specs=[WHOLE] * sum(counts),
        out_specs=ANYWHERE,
        scratch_shapes=[
            pltpu.VMEM((4, bands, bands), jnp.float32),
            pltpu.SemaphoreType.DMA((4,)),
        ],
        compiler_params=pltpu.CompilerParams(vmem_limit_bytes=16 * MIB),
        cost_estimate=pl.CostEstimate(flops=0, bytes_accessed=1024, transcendentals=0),
        name="assemble",
    )(*[array for part in parts for array in part])


def local(coefficients, shifts):
    bands, width = coefficients.shape[2:]
    unit = bands // sum(SIXTEENTHS)
    edges = [0]
    for size in SIXTEENTHS:
        edges.append(edges[-1] + size * unit)
    late = width // PWB * 3 // 4 * PWB
    coefficients = pltpu.with_memory_space_constraint(coefficients, pltpu.HBM)
    ranges = [(chunk, 0, width) for chunk in range(5)] + [(5, 0, late), (5, late, width)]
    blocks = []
    for chunk, low, high in ranges:
        some = slice(edges[chunk], edges[chunk + 1])
        blocks.append(cut(coefficients, some, slice(low, high), *blocks[-1:]))
    placed = placed_bands(coefficients, shifts, *blocks[-1:])
    placed = pltpu.with_memory_space_constraint(placed, pltpu.VMEM)
    arrived = [moved(block, "ka", -1) for block in blocks[:3]]
    whole = []
    for chunk in range(5):
        waiting = [[], blocks[3:4], blocks[4:5], blocks[5:7], []][chunk]
        partial = correlate(placed, arrived[chunk], *whole[-1:], held=waiting)
        if waiting:
            partial, *waiting = partial
            arrived.extend(moved(block, "ka", -1) for block in waiting)
        whole.append(summed_over_pw(partial))
    most = jnp.concatenate(whole, axis=1)
    last, most = correlate(placed, arrived[5], held=[most])
    most_before = moved(most, "ka", 1)
    last = correlate(placed, arrived[6], first=late, begun=last)
    return assembled([most], [most_before], *sums_here_and_next(last))


def solution(mesh):
    return jax.shard_map(
        local,
        mesh=mesh,
        in_specs=(P(("groups", "ka"), None, None, "pw"), P(("groups", "ka"), None, "pw")),
        out_specs=P(("groups", "ka"), None, None, None, None),
        check_vma=False,
    )
```
